32 devices in a mesh: seq: 8 (over z, core), head: 4 (over y, x).
Axes of the slice: x: 2, y: 2, z: 4, core: 2. Of those that a mesh axis runs over, the one named last changes fastest.
Arguments:
- tokens: bfloat16 [64, 512, 1024], P('seq'), may hold values from -36 to 36
- lengths: int32 [64], P('seq'), may hold values from 1 to 512, 16384 in all
- attn_in: float32 [1024, 3, 1024], P(('seq', 'head')), may hold values from -0.4 to 0.4
- attn_out: float32 [1024, 1024], P(None, ('seq', 'head')), may hold values from -0.1875 to 0.1875
- mlp_in: float32 [1024, 4096], P(('seq', 'head')), may hold values from -0.1875 to 0.1875
- mlp_out: float32 [4096, 1024], P(None, ('seq', 'head')), may hold values from -0.09375 to 0.09375
- norm_gain: float32 [2, 1024], replicated, may hold values from 0.5 to 1.5
- norm_shift: float32 [2, 1024], replicated, may hold values from -3 to 3
Outputs:
- encoded: bfloat16 [64, 512, 1024], P('seq', 'head')
- key_cache: bfloat16 [64, 512, 1024], P('seq', None, 'head')
- value_cache: bfloat16 [64, 512, 1024], P('seq', None, 'head')
The draws below stay inside these ranges and needn't reach their ends.
Inputs may be any that keep to these rules, and one draw needn't show every extreme that they name: `lengths`: some prompt has exactly 512 tokens.
All inputs are finite; a program needn't handle non-finite values. No bound on the sum of `lengths` on one device may be relied on, other than what follows from the above.
Results may differ from the reference program's by a relative error of at most 0.02.
Values may be sent and summed in bfloat16 or wider, within the bound.
No kernel may reach another device: no remote copies, remote signals or barrier semaphores. Data moves between devices by JAX's collectives and lax.ppermute only.
A program may use at most 128 MiB of HBM per device.

```python
import math
import jax
import jax.numpy as jnp
import numpy as np
from jax import lax

D = 1024
H = 16
FF = 4096
DH = 64
LEN = 512
PROMPTS = 64
N_HEAD = 4


def draw_tokens(key, part):
    keys = jax.random.split(key, 3)
    base = jnp.clip(jax.random.normal(keys[0], (PROMPTS, LEN, D), jnp.float32), -3.0, 3.0)
    row_scale = jnp.exp(jax.random.uniform(keys[1], (PROMPTS, LEN, 1), jnp.float32, math.log(0.4), math.log(4.0)))
    col_scale = jnp.exp(jax.random.uniform(keys[2], (1, 1, D), jnp.float32, math.log(0.3), math.log(3.0)))
    field = base * row_scale * col_scale
    return field.astype(jnp.bfloat16)


def draw_attn_in(key, part):
    keys = jax.random.split(key, 3)
    scale_factor = 1.0 / math.sqrt(D)
    query_part = jnp.clip(jax.random.normal(keys[0], (D, D), jnp.float32), -4.0, 4.0) * scale_factor
    key_part = jnp.clip(jax.random.normal(keys[1], (D, D), jnp.float32), -4.0, 4.0) * scale_factor
    value_part = jnp.clip(jax.random.normal(keys[2], (D, D), jnp.float32), -4.0, 4.0) * scale_factor
    return jnp.stack([query_part, key_part, value_part], axis=1)


def block_levels(rng, shape, cuts, low, high):
    level = 1.0
    for axis_at, blocks in cuts:
        draws = jax.random.uniform(jax.random.fold_in(jax.random.fold_in(rng, 6), axis_at), (blocks,), jnp.float32, low / len(cuts), high / len(cuts))
        level = level * jnp.repeat(jnp.exp(draws), shape[axis_at] // blocks).reshape((-1,) + (1,) * (len(shape) - 1 - axis_at))
    return level


def length_profile(amount, total, limit, skew):
    weights = [(1 << 20) // math.isqrt(rank ** skew) + 1 for rank in range(2, amount + 1)]
    surplus, given = total - limit - (amount - 1), [1] * (amount - 1)
    while surplus > 0:
        free = [i for i in range(amount - 1) if given[i] < limit]
        mass, budget = sum([weights[i] for i in free]), surplus
        for i in free:
            addition = min(limit - given[i], max(1, budget * weights[i] // mass), surplus)
            given[i] = given[i] + addition
            surplus = surplus - addition
    return np.array([limit] + given)


def uneven(own_key, number_of, total, most, skew):
    if number_of == 2:
        one = jax.random.randint(own_key, (), max(1, total - most), min(most, total - 1) + 1)
        return jnp.stack([one, total - one])
    sizes = jnp.asarray(length_profile(number_of, total, most, skew), jnp.int32)
    twos = (number_of - 1) // 2
    giver, taker = sizes[1:1 + 2 * twos:2], sizes[2:2 + 2 * twos:2]
    margin = jnp.minimum(giver - 1, most - taker)
    shifted = jax.random.randint(jax.random.fold_in(own_key, 1), (twos,), 0, 1 << 20) % (margin + 1)
    sizes = sizes.at[1:1 + 2 * twos:2].set(giver - shifted).at[2:2 + 2 * twos:2].set(taker + shifted)
    return sizes[jax.random.permutation(jax.random.fold_in(own_key, 2), number_of)]


def noise(stream_key, shape, deviation, bound, cuts=(), held_as=jnp.bfloat16):
    drawn = deviation * jax.random.normal(stream_key, shape, jnp.float32)
    if cuts:
        drawn = drawn * block_levels(stream_key, shape, cuts, -0.22, 0.18)
    return jnp.clip(drawn, -bound, bound).astype(held_as)


def setup_inputs(seed: int = 0) -> dict:
    seeds = jax.random.split(jax.random.key(seed), 9)
    return {
        "tokens": draw_tokens(jax.random.fold_in(seeds[8], 71), 0),
        "lengths": uneven(seeds[1], PROMPTS, PROMPTS * LEN // 2, LEN, 2).astype(jnp.int32),
        "attn_in": draw_attn_in(jax.random.fold_in(seeds[8], 71), 0),
        "attn_out": noise(seeds[3], (D, D), D ** -0.5, 0.1875, ((1, 32),), jnp.float32),
        "mlp_in": noise(seeds[4], (D, FF), D ** -0.5, 0.1875, ((0, 32),), jnp.float32),
        "mlp_out": noise(seeds[5], (FF, D), FF ** -0.5, 0.09375, ((1, 32),), jnp.float32),
        "norm_gain": jnp.clip(1.0 + 0.1 * jax.random.normal(seeds[6], (2, D), jnp.float32), 0.5, 1.5),
        "norm_shift": noise(seeds[7], (2, D), 0.5, 3.0, (), jnp.float32),
    }


EPSILON = 1e-05

def layer_norm(values, gain, shift):
    center = values - lax.optimization_barrier(jnp.mean(values, axis=-1, keepdims=True))
    spread = lax.optimization_barrier(jnp.mean(center * center, axis=-1, keepdims=True))
    return center * lax.rsqrt(spread + EPSILON) * gain + shift

def block_sum(left_side, right_side, blocks):
    block_cols = left_side.shape[1] // blocks
    summed = jnp.zeros((left_side.shape[0], right_side.shape[1]), jnp.float32)
    for block_index in range(blocks):
        lower = block_index * block_cols
        partial_sum = jnp.dot(left_side[:, lower:lower + block_cols], right_side[lower:lower + block_cols], preferred_element_type=jnp.float32)
        rounded = lax.optimization_barrier(partial_sum.astype(jnp.bfloat16))
        summed = summed + rounded.astype(jnp.float32)
    return summed

def reference(tokens, lengths, attn_in, attn_out, mlp_in, mlp_out, norm_gain, norm_shift):
    qkv_weight = attn_in.astype(jnp.bfloat16).reshape(D, 3 * D)
    proj_weight = attn_out.astype(jnp.bfloat16)
    up_weight = mlp_in.astype(jnp.bfloat16)
    down_weight = mlp_out.astype(jnp.bfloat16)
    scale_factor = 1.0 / math.sqrt(DH)
    positions = jnp.arange(LEN, dtype=jnp.int32)

    def encode_prompt(operands):
        prompt_tokens, prompt_length = operands
        inside = positions < prompt_length
        projected = jnp.dot(prompt_tokens, qkv_weight, preferred_element_type=jnp.float32).astype(jnp.bfloat16)
        projected = projected.reshape(LEN, 3, H, DH)
        queries = projected[:, 0].astype(jnp.float32)
        key_heads = projected[:, 1].astype(jnp.float32)
        value_heads = projected[:, 2].astype(jnp.float32)
        scores = jnp.einsum('qhd,khd->hqk', queries, key_heads) * scale_factor
        scores = jnp.where(inside[None, None, :], scores, -1e+30)
        row_peak = lax.optimization_barrier(jnp.max(scores, axis=-1, keepdims=True))
        raised = jnp.exp(scores - row_peak)
        weights = (raised / lax.optimization_barrier(jnp.sum(raised, axis=-1, keepdims=True))).astype(jnp.bfloat16)
        context = jnp.einsum('hqk,khd->qhd', weights.astype(jnp.float32), value_heads)
        context = context.astype(jnp.bfloat16).reshape(LEN, D)
        attended = block_sum(context, proj_weight, N_HEAD)
        normed = layer_norm(prompt_tokens.astype(jnp.float32) + attended, norm_gain[0], norm_shift[0]).astype(jnp.bfloat16)
        hidden = jax.nn.gelu(jnp.dot(normed, up_weight, preferred_element_type=jnp.float32), approximate=False).astype(jnp.bfloat16)
        mixed = block_sum(hidden, down_weight, N_HEAD)
        finished = layer_norm(normed.astype(jnp.float32) + mixed, norm_gain[1], norm_shift[1])
        row_mask = inside[:, None]
        encoded = jnp.where(row_mask, finished, 0.0).astype(jnp.bfloat16)
        key_rows = projected[:, 1].reshape(LEN, D)
        value_rows = projected[:, 2].reshape(LEN, D)
        key_cache = jnp.where(row_mask, key_rows, jnp.zeros_like(key_rows))
        value_cache = jnp.where(row_mask, value_rows, jnp.zeros_like(value_rows))
        return (encoded, key_cache, value_cache)
    encoded, key_cache, value_cache = lax.map(encode_prompt, (tokens, lengths))
    return (encoded, key_cache, value_cache)
```

```python
import functools
import math

import jax
import jax.numpy as jnp
from jax import lax
from jax.experimental import pallas as pl
from jax.experimental.pallas import tpu as pltpu
from jax.sharding import PartitionSpec as P

DH = 64
EPSILON = 1e-05
TILE = 128
NT = (((1,), (1,)), ((), ()))
MIB = 1024 * 1024


def swap_seq(x, k):
    return lax.ppermute(x, "seq", [(i, i ^ k) for i in range(lax.axis_size("seq"))])


def swap_head(x, k):
    return lax.ppermute(x, "head", [(i, i ^ k) for i in range(lax.axis_size("head"))])


def gather_all(x):
    depths = list(range(0, lax.axis_size("seq"), 2))
    half = len(depths) // 2
    blocks = []
    for depth_list, first, second in ((depths[:half], 1, 2), (depths[half:], 2, 1)):
        own = jnp.concatenate([x if k == 0 else swap_seq(x, k) for k in depth_list], axis=0)
        one = swap_head(own, first)
        two = swap_head(own, second)
        both = swap_head(one, second)
        for block, h in ((own, 0), (one, first), (two, second), (both, 3)):
            blocks.append((block, [(k, h) for k in depth_list]))
    return blocks + [(swap_seq(b, 1), [(s ^ 1, h) for s, h in at]) for b, at in blocks]


def shard_copies(refs, places, place_ref, heads_axis, rows, columns, target, sem):
    copies = []
    for ref, at in zip(refs, places):
        for n, (s, h) in enumerate(at):
            index = (place_ref[0] ^ s) * heads_axis + (place_ref[1] ^ h)
            copies.append(
                pltpu.make_async_copy(
                    ref.at[pl.ds(n * rows, rows), pl.ds(columns[0], columns[1])],
                    target.at[pl.ds(pl.multiple_of(index * rows, rows), rows), :],
                    sem.at[len(copies)],
                )
            )
    return copies


def attention_kernel(places, heads_axis, rows, *refs):
    lengths_ref, place_ref, tokens_ref = refs[:3]
    weight_refs = refs[3 : 3 + len(places)]
    key_ref, value_ref = refs[3 + len(places) : 5 + len(places)]
    context_refs = refs[5 + len(places) : 5 + len(places) + heads_axis]
    weight, held, sem = refs[5 + len(places) + heads_axis :]
    prompt = pl.program_id(0)
    width = key_ref.shape[2]
    seq_len = key_ref.shape[1]
    row_count = context_refs[0].shape[1]

    @pl.when(prompt == 0)
    def _():
        copies = []
        for n, (ref, s) in enumerate(zip(weight_refs, places)):
            start = pl.multiple_of((place_ref[0] ^ s) * rows, rows)
            copies.append(pltpu.make_async_copy(ref, weight.at[pl.ds(start, rows), :], sem.at[n]))
        for copy in copies:
            copy.start()
        for copy in copies:
            copy.wait()

    length = lengths_ref[prompt]
    filled = (length + TILE - 1) // TILE
    lanes = lax.broadcasted_iota(jnp.int32, (1, width), 1) // DH

    def part(tiles):
        span = tiles * TILE
        projected = jnp.dot(tokens_ref[0, :span, :], weight[...], preferred_element_type=jnp.float32)
        queries = (projected[:, :width] * (math.log2(math.e) / math.sqrt(DH))).astype(jnp.bfloat16)
        keys = projected[:, width : 2 * width].astype(jnp.bfloat16)
        values = projected[:, 2 * width :].astype(jnp.bfloat16)
        inside = lax.broadcasted_iota(jnp.int32, (span, 1), 0) < length
        key_ref[0, :span, :] = jnp.where(inside, keys, jnp.zeros_like(keys))
        value_ref[0, :span, :] = jnp.where(inside, values, jnp.zeros_like(values))
        if span < seq_len:
            rest = jnp.zeros((seq_len - span, width), jnp.bfloat16)
            key_ref[0, span:, :] = rest
            value_ref[0, span:, :] = rest
            held[span:, :] = rest
        column = lax.broadcasted_iota(jnp.int32, (1, span), 1) < length
        context = jnp.zeros((span, width), jnp.float32)
        for head in range(width // DH):
            mine = lanes == head
            query = jnp.where(mine, queries, jnp.zeros_like(queries))
            scores = lax.dot_general(query, keys, NT, preferred_element_type=jnp.float32)
            scores = jnp.where(column, scores, -1e30)
            raised = jnp.exp2(scores - jnp.max(scores, axis=-1, keepdims=True))
            total = jnp.sum(raised, axis=-1, keepdims=True)
            out = jnp.dot(raised.astype(jnp.bfloat16), values, preferred_element_type=jnp.float32)
            context = jnp.where(mine, out * (1.0 / total), context)
        held[:span, :] = context.astype(jnp.bfloat16)

    for tiles in range(1, seq_len // TILE + 1):
        pl.when(filled == tiles)(functools.partial(part, tiles))
    for k, ref in enumerate(context_refs):
        start = pl.multiple_of((place_ref[1] ^ k) * row_count, row_count)
        ref[0] = held[pl.ds(start, row_count), :]


def attention(lengths, place, tokens, weight_blocks, heads_axis):
    prompts, seq_len, model_width = tokens.shape
    width = model_width // heads_axis
    row_count = seq_len // heads_axis
    rows = weight_blocks[0][0].shape[0]
    cache = jax.ShapeDtypeStruct((prompts, seq_len, width), jnp.bfloat16)
    piece = jax.ShapeDtypeStruct((prompts, row_count, width), jnp.bfloat16)
    by_prompt = lambda p, *_: (p, 0, 0)
    return pl.pallas_call(
        functools.partial(attention_kernel, [s for _, s in weight_blocks], heads_axis, rows),
        out_shape=[cache, cache] + [piece] * heads_axis,
        grid_spec=pltpu.PrefetchScalarGridSpec(
            num_scalar_prefetch=2,
            grid=(prompts,),
            in_specs=[pl.BlockSpec((1, seq_len, model_width), by_prompt)]
            + [pl.BlockSpec(memory_space=pl.ANY)] * len(weight_blocks),
            out_specs=[pl.BlockSpec((1, seq_len, width), by_prompt)] * 2
            + [pl.BlockSpec((1, row_count, width), by_prompt)] * heads_axis,
            scratch_shapes=[
                pltpu.VMEM((model_width, 3 * width), jnp.bfloat16),
                pltpu.VMEM((seq_len, width), jnp.bfloat16),
                pltpu.SemaphoreType.DMA((len(weight_blocks),)),
            ],
        ),
        compiler_params=pltpu.CompilerParams(vmem_limit_bytes=40 * MIB),
        cost_estimate=pl.CostEstimate(
            flops=2 * prompts * seq_len * model_width * 3 * width + 8 * prompts * seq_len * seq_len * width,
            bytes_accessed=4 * prompts * seq_len * model_width,
            transcendentals=prompts * seq_len * seq_len * width // DH,
        ),
        name="attention",
    )(lengths, place, tokens, *[block for block, _ in weight_blocks])


def normalize(values, gain, shift):
    center = values - jnp.mean(values, axis=-1, keepdims=True)
    spread = jnp.mean(center * center, axis=-1, keepdims=True)
    return center * lax.rsqrt(spread + EPSILON) * gain + shift


def project_kernel(places, heads_axis, rows, *refs):
    place_ref, tokens_ref = refs[:2]
    context_refs = refs[2 : 2 + heads_axis]
    weight_refs = refs[2 + heads_axis : 2 + heads_axis + len(places)]
    gain_ref, shift_ref, out_ref, weight, sem = refs[2 + heads_axis + len(places) :]

    @pl.when(pl.program_id(0) == 0)
    def _():
        copies = shard_copies(
            weight_refs, places, place_ref, heads_axis, rows, (0, weight.shape[1]), weight, sem
        )
        for copy in copies:
            copy.start()
        for copy in copies:
            copy.wait()

    count = out_ref.shape[0] * out_ref.shape[1]
    model_width = out_ref.shape[2]
    total = tokens_ref[...].reshape(count, model_width).astype(jnp.float32)
    for k, ref in enumerate(context_refs):
        width = ref.shape[2]
        start = pl.multiple_of((place_ref[1] ^ k) * width, width)
        total = total + lax.dot_general(
            ref[...].reshape(count, width),
            weight[:, pl.ds(start, width)],
            NT,
            preferred_element_type=jnp.float32,
        )
    normed = normalize(total, gain_ref[0:1, :], shift_ref[0:1, :])
    out_ref[...] = normed.astype(jnp.bfloat16).reshape(out_ref.shape)


def project(place, tokens, contexts, blocks, gain, shift, rows, steps):
    prompts, seq_len, model_width = tokens.shape
    heads_axis = len(contexts)
    row_count, width = contexts[0].shape[1:]
    group = prompts // steps
    places = [at for _, at in blocks]
    copies = sum(len(at) for at in places)
    return pl.pallas_call(
        functools.partial(project_kernel, places, heads_axis, rows),
        out_shape=jax.ShapeDtypeStruct((prompts, row_count, model_width), jnp.bfloat16),
        grid_spec=pltpu.PrefetchScalarGridSpec(
            num_scalar_prefetch=1,
            grid=(steps,),
            in_specs=[pl.BlockSpec((group, row_count, model_width), lambda p, place: (p, place[1], 0))]
            + [pl.BlockSpec((group, row_count, width), lambda p, place: (p, 0, 0))] * heads_axis
            + [pl.BlockSpec(memory_space=pl.ANY)] * len(blocks)
            + [pl.BlockSpec(gain.shape, lambda p, place: (0, 0))] * 2,
            out_specs=pl.BlockSpec((group, row_count, model_width), lambda p, place: (p, 0, 0)),
            scratch_shapes=[
                pltpu.VMEM((model_width, model_width), jnp.bfloat16),
                pltpu.SemaphoreType.DMA((copies,)),
            ],
        ),
        compiler_params=pltpu.CompilerParams(vmem_limit_bytes=40 * MIB),
        cost_estimate=pl.CostEstimate(
            flops=2 * prompts * row_count * model_width * model_width,
            bytes_accessed=8 * prompts * row_count * model_width,
            transcendentals=0,
        ),
        name="project",
    )(place, tokens, *contexts, *[block for block, _ in blocks], gain, shift)


def expand_kernel(places, heads_axis, rows, start_column, *refs):
    place_ref, normed_ref = refs[:2]
    weight_refs = refs[2 : 2 + len(places)]
    out_ref, weight, product, sem = refs[2 + len(places) :]
    step = pl.program_id(0)
    last = pl.num_programs(0) - 1
    chunk = out_ref.shape[1]

    @pl.when(step == 0)
    def _():
        copies = shard_copies(
            weight_refs, places, place_ref, heads_axis, rows, (start_column, weight.shape[1]), weight, sem
        )
        for copy in copies:
            copy.start()
        for copy in copies:
            copy.wait()

    def multiply():
        at = pl.multiple_of(step * chunk, chunk)
        product[lax.rem(step, 2)] = jnp.dot(
            normed_ref[...], weight[:, pl.ds(at, chunk)], preferred_element_type=jnp.float32
        )

    def activate():
        values = product[lax.rem(step + 1, 2)]
        out_ref[...] = (0.5 * values * (1.0 + lax.erf(values * math.sqrt(0.5)))).astype(jnp.bfloat16)

    @pl.when(step == 0)
    def _():
        multiply()

    @pl.when((step > 0) & (step < last))
    def _():
        multiply()
        activate()

    @pl.when(step == last)
    def _():
        activate()


def expand(place, normed, blocks, rows, start_column, hidden_width, heads_axis, chunk):
    count, model_width = normed.shape
    places = [at for _, at in blocks]
    copies = sum(len(at) for at in places)
    steps = hidden_width // chunk
    return pl.pallas_call(
        functools.partial(expand_kernel, places, heads_axis, rows, start_column),
        out_shape=jax.ShapeDtypeStruct((count, hidden_width), jnp.bfloat16),
        grid_spec=pltpu.PrefetchScalarGridSpec(
            num_scalar_prefetch=1,
            grid=(steps + 1,),
            in_specs=[pl.BlockSpec((count, model_width), lambda n, place: (0, 0))]
            + [pl.BlockSpec(memory_space=pl.ANY)] * len(blocks),
            out_specs=pl.BlockSpec((count, chunk), lambda n, place: (0, jnp.maximum(n - 1, 0))),
            scratch_shapes=[
                pltpu.VMEM((model_width, hidden_width), jnp.bfloat16),
                pltpu.VMEM((2, count, chunk), jnp.float32),
                pltpu.SemaphoreType.DMA((copies,)),
            ],
        ),
        compiler_params=pltpu.CompilerParams(vmem_limit_bytes=48 * MIB),
        cost_estimate=pl.CostEstimate(
            flops=2 * count * model_width * hidden_width,
            bytes_accessed=2 * (count + model_width) * hidden_width,
            transcendentals=count * hidden_width,
        ),
        name="expand",
    )(place, normed, *[block for block, _ in blocks])


def contract_kernel(lengths_ref, place_ref, hidden_ref, weight_ref, normed_ref, gain_ref, shift_ref, out_ref, total):
    step = pl.program_id(0)
    partial = lax.dot_general(hidden_ref[...], weight_ref[...], NT, preferred_element_type=jnp.float32)

    @pl.when(step == 0)
    def _():
        total[...] = partial

    @pl.when(step > 0)
    def _():
        total[...] += partial

    @pl.when(step == pl.num_programs(0) - 1)
    def _():
        prompts, row_count, _ = out_ref.shape
        for p in range(prompts):
            rows = slice(p * row_count, (p + 1) * row_count)
            finished = normalize(
                normed_ref[rows, :].astype(jnp.float32) + total[rows, :], gain_ref[1:2, :], shift_ref[1:2, :]
            )
            position = place_ref[1] * row_count + lax.broadcasted_iota(jnp.int32, (row_count, 1), 0)
            out_ref[p] = jnp.where(position < lengths_ref[p], finished, 0.0).astype(jnp.bfloat16)


def contract(lengths, place, hidden, weight, normed, gain, shift, prompts, steps):
    count, model_width = normed.shape
    chunk = hidden.shape[1] // steps
    row_count = count // prompts
    return pl.pallas_call(
        contract_kernel,
        out_shape=jax.ShapeDtypeStruct((prompts, row_count, model_width), jnp.bfloat16),
        grid_spec=pltpu.PrefetchScalarGridSpec(
            num_scalar_prefetch=2,
            grid=(steps,),
            in_specs=[
                pl.BlockSpec((count, chunk), lambda n, *_: (0, n)),
                pl.BlockSpec((model_width, chunk), lambda n, *_: (0, n)),
                pl.BlockSpec((count, model_width), lambda n, *_: (0, 0)),
                pl.BlockSpec(gain.shape, lambda n, *_: (0, 0)),
                pl.BlockSpec(gain.shape, lambda n, *_: (0, 0)),
            ],
            out_specs=pl.BlockSpec((prompts, row_count, model_width), lambda n, *_: (0, 0, 0)),
            scratch_shapes=[pltpu.VMEM((count, model_width), jnp.float32)],
        ),
        compiler_params=pltpu.CompilerParams(vmem_limit_bytes=48 * MIB),
        cost_estimate=pl.CostEstimate(
            flops=2 * count * model_width * hidden.shape[1],
            bytes_accessed=2 * (count + model_width) * hidden.shape[1],
            transcendentals=0,
        ),
        name="contract",
    )(lengths, place, hidden, weight, normed, gain, shift)


def shards(tokens, lengths, attn_in, attn_out, mlp_in, mlp_out, norm_gain, norm_shift):
    heads_axis = lax.axis_size("head")
    prompts, seq_len, model_width = tokens.shape
    hidden_width = mlp_in.shape[1]
    width = model_width // heads_axis
    row_count = seq_len // heads_axis
    rows = mlp_in.shape[0]
    place = jnp.stack([lax.axis_index("seq"), lax.axis_index("head")]).astype(jnp.int32)

    down_weight = lax.all_gather(mlp_out.T.astype(jnp.bfloat16), ("seq", "head"), axis=0, tiled=True)

    in_cast = attn_in.astype(jnp.bfloat16).reshape(rows, 3, heads_axis, width)
    in_cast = in_cast.transpose(2, 0, 1, 3).reshape(heads_axis, rows, 3 * width)
    in_rows = lax.all_to_all(in_cast, "head", 0, 0).reshape(heads_axis * rows, 3 * width)
    in_blocks = [(in_rows if s == 0 else swap_seq(in_rows, s), s) for s in range(0, lax.axis_size("seq"), 2)]
    in_blocks = in_blocks + [(swap_seq(block, 1), s ^ 1) for block, s in in_blocks]

    out_up = jnp.concatenate([attn_out.T, mlp_in], axis=1).astype(jnp.bfloat16)
    blocks = gather_all(out_up)

    key_cache, value_cache, *contexts = attention(lengths, place, tokens, in_blocks, heads_axis)
    contexts = [contexts[0]] + [swap_head(contexts[k], k) for k in range(1, heads_axis)]
    normed = project(place, tokens, contexts, blocks, norm_gain, norm_shift, rows, 2)
    normed = normed.reshape(prompts * row_count, model_width)
    hidden = expand(place, normed, blocks, rows, model_width, hidden_width, heads_axis, 512)
    encoded = contract(lengths, place, hidden, down_weight, normed, norm_gain, norm_shift, prompts, 4)
    return (encoded, key_cache, value_cache)


def solution(mesh):
    in_specs = (
        P("seq", None, None),
        P("seq"),
        P(("seq", "head"), None, None),
        P(None, ("seq", "head")),
        P(("seq", "head"), None),
        P(None, ("seq", "head")),
        P(),
        P(),
    )
    out_specs = (P("seq", "head", None), P("seq", None, "head"), P("seq", None, "head"))
    return jax.shard_map(shards, mesh=mesh, in_specs=in_specs, out_specs=out_specs, check_vma=False)
```

```python
import functools
import math

import jax
import jax.numpy as jnp
from jax import lax
from jax.experimental import pallas as pl
from jax.experimental.pallas import tpu as pltpu
from jax.sharding import PartitionSpec as P

DH = 64
EPSILON = 1e-05
TILE = 128
NT = (((1,), (1,)), ((), ()))
MIB = 1024 * 1024
ATTENTION_CALLS = 1


def swap_seq(x, k):
    return lax.ppermute(x, "seq", [(i, i ^ k) for i in range(lax.axis_size("seq"))])


def swap_head(x, k):
    return lax.ppermute(x, "head", [(i, i ^ k) for i in range(lax.axis_size("head"))])


def depths():
    return list(range(0, lax.axis_size("seq"), 2))


def after(x, *done):
    return lax.optimization_barrier((x, done))[0]


def along_depth(x):
    groups = [[d + core for d in depths()] for core in range(2)]
    return lax.all_gather(x, "seq", axis=0, tiled=True, axis_index_groups=groups)


def by_depth(x):
    return [x] + [swap_seq(x, k) for k in depths()[1:]]


def across_first(parts):
    half = len(parts) // 2
    lower, upper = jnp.concatenate(parts[:half], axis=0), jnp.concatenate(parts[half:], axis=0)
    return [[lower, swap_head(lower, 1), swap_head(lower, 2)], [upper, swap_head(upper, 2), swap_head(upper, 1)]]


def across_second(first):
    half = len(depths()) // 2
    blocks = []
    for (own, one, two), (a, b), at in zip(first, ((1, 2), (2, 1)), (depths()[:half], depths()[half:])):
        for block, h in ((own, 0), (one, a), (two, b), (swap_head(one, b), 3)):
            blocks.append((block, [(-1, s, h) for s in at]))
    return blocks


def cycle():
    seq = list(range(lax.axis_size("seq")))
    order = []
    for n in range(len(seq) // 2):
        for h in across_order()[:: 1 if n % 2 == 0 else -1]:
            order.extend([(2 * n, h), (2 * n + 1, h)])
    return order


def across_order():
    return [n ^ (n >> 1) for n in range(lax.axis_size("head"))]


def gather_cycle(x):
    heads = lax.axis_size("head")
    group = [s * heads + h for s, h in cycle()]
    return lax.all_gather(x, ("seq", "head"), axis=0, tiled=True, axis_index_groups=[group])


def other_core(blocks):
    return blocks + [(swap_seq(b, 1), [(m, s ^ 1, h) for m, s, h in at]) for b, at in blocks]


def shard_copies(refs, places, place_ref, heads_axis, rows, start, target, sem):
    copies = []
    for ref, at in zip(refs, places):
        for n, (mask, s, h) in enumerate(at):
            index = s * heads_axis + h if mask is None else (place_ref[0] & mask ^ s) * heads_axis + (place_ref[1] ^ h)
            copies.append(
                pltpu.make_async_copy(
                    ref.at[pl.ds(n * rows, rows), pl.ds(start, target.shape[1])],
                    target.at[pl.ds(index * rows if mask is None else pl.multiple_of(index * rows, rows), rows), :],
                    sem.at[len(copies)],
                )
            )
    return copies


def attention_kernel(places, heads_axis, rows, first, aliases, *refs):
    lengths_ref, place_ref, tokens_ref = refs[:3]
    weight_refs = refs[3 : 3 + len(places)]
    refs = refs[:3] + weight_refs + refs[3 + len(places) + aliases :]
    key_ref, value_ref = refs[3 + len(places) : 5 + len(places)]
    context_refs = refs[5 + len(places) : 5 + len(places) + heads_axis]
    weight, held, sem = refs[5 + len(places) + heads_axis :]
    prompt = pl.program_id(0)
    width = key_ref.shape[2]
    seq_len = key_ref.shape[1]
    row_count = context_refs[0].shape[1]

    @pl.when(prompt == 0)
    def _():
        copies = []
        for core, ref in zip(places, weight_refs):
            for depth in range(ref.shape[0] // rows):
                start = pl.multiple_of((place_ref[0] ^ (2 * depth + core)) * rows, rows)
                copies.append(
                    pltpu.make_async_copy(
                        ref.at[pl.ds(depth * rows, rows), :],
                        weight.at[pl.ds(start, rows), :],
                        sem.at[len(copies)],
                    )
                )
        for copy in copies:
            copy.start()
        for copy in copies:
            copy.wait()

    length = lengths_ref[first + prompt]
    filled = (length + TILE - 1) // TILE
    lanes = lax.broadcasted_iota(jnp.int32, (1, width), 1) // DH

    def part(tiles):
        span = tiles * TILE
        projected = jnp.dot(tokens_ref[0, :span, :], weight[...], preferred_element_type=jnp.float32)
        queries = (projected[:, :width] * (math.log2(math.e) / math.sqrt(DH))).astype(jnp.bfloat16)
        keys = projected[:, width : 2 * width].astype(jnp.bfloat16)
        values = projected[:, 2 * width :].astype(jnp.bfloat16)
        inside = lax.broadcasted_iota(jnp.int32, (span, 1), 0) < length
        key_ref[0, :span, :] = jnp.where(inside, keys, jnp.zeros_like(keys))
        value_ref[0, :span, :] = jnp.where(inside, values, jnp.zeros_like(values))
        if span < seq_len:
            rest = jnp.zeros((seq_len - span, width), jnp.bfloat16)
            key_ref[0, span:, :] = rest
            value_ref[0, span:, :] = rest
            held[span:, :] = rest
        column = lax.broadcasted_iota(jnp.int32, (1, span), 1) < length
        context = jnp.zeros((span, width), jnp.float32)
        for head in range(width // DH):
            mine = lanes == head
            query = jnp.where(mine, queries, jnp.zeros_like(queries))
            scores = lax.dot_general(query, keys, NT, preferred_element_type=jnp.float32)
            scores = jnp.where(column, scores, -1e30)
            raised = jnp.exp2(scores - jnp.max(scores, axis=-1, keepdims=True))
            total = jnp.sum(raised, axis=-1, keepdims=True)
            out = jnp.dot(raised.astype(jnp.bfloat16), values, preferred_element_type=jnp.float32)
            context = jnp.where(mine, out * (1.0 / total), context)
        held[:span, :] = context.astype(jnp.bfloat16)

    for tiles in range(1, seq_len // TILE + 1):
        pl.when(filled == tiles)(functools.partial(part, tiles))
    for k, ref in enumerate(context_refs):
        start = pl.multiple_of((place_ref[1] ^ k) * row_count, row_count)
        ref[0] = held[pl.ds(start, row_count), :]


def attention(lengths, place, tokens, weight_blocks, heads_axis, first, count, caches):
    prompts, seq_len, model_width = tokens.shape
    width = model_width // heads_axis
    row_count = seq_len // heads_axis
    rows = model_width // lax.axis_size("seq")
    cache = jax.ShapeDtypeStruct((prompts, seq_len, width), jnp.bfloat16)
    piece = jax.ShapeDtypeStruct((count, row_count, width), jnp.bfloat16)
    by_prompt = lambda p, *_: (p, 0, 0)
    shifted = lambda p, *_: (first + p, 0, 0)
    return pl.pallas_call(
        functools.partial(attention_kernel, [s for _, s in weight_blocks], heads_axis, rows, first, len(caches)),
        out_shape=[cache, cache] + [piece] * heads_axis,
        grid_spec=pltpu.PrefetchScalarGridSpec(
            num_scalar_prefetch=2,
            grid=(count,),
            in_specs=[pl.BlockSpec((1, seq_len, model_width), shifted)]
            + [pl.BlockSpec(memory_space=pl.ANY)] * (len(weight_blocks) + len(caches)),
            out_specs=[pl.BlockSpec((1, seq_len, width), shifted)] * 2
            + [pl.BlockSpec((1, row_count, width), by_prompt)] * heads_axis,
            scratch_shapes=[
                pltpu.VMEM((model_width, 3 * width), jnp.bfloat16),
                pltpu.VMEM((seq_len, width), jnp.bfloat16),
                pltpu.SemaphoreType.DMA((model_width // rows,)),
            ],
        ),
        input_output_aliases={3 + len(weight_blocks) + n: n for n in range(len(caches))},
        compiler_params=pltpu.CompilerParams(vmem_limit_bytes=62 * MIB),
        cost_estimate=pl.CostEstimate(
            flops=2 * count * seq_len * model_width * 3 * width + 8 * count * seq_len * seq_len * width,
            bytes_accessed=4 * count * seq_len * model_width,
            transcendentals=count * seq_len * seq_len * width // DH,
        ),
        name="attention",
    )(lengths, place, tokens, *[block for block, _ in weight_blocks], *caches)


def normalize(values, gain, shift):
    center = values - jnp.mean(values, axis=-1, keepdims=True)
    spread = jnp.mean(center * center, axis=-1, keepdims=True)
    return center * lax.rsqrt(spread + EPSILON) * gain + shift


def project_kernel(places, heads_axis, rows, start_column, *refs):
    place_ref, tokens_ref = refs[:2]
    halves = (len(refs) - 2 - len(places) - 5) // heads_axis
    context_refs = refs[2 : 2 + halves * heads_axis]
    weight_refs = refs[2 + halves * heads_axis : 2 + halves * heads_axis + len(places)]
    gain_ref, shift_ref, out_ref, weight, sem = refs[2 + halves * heads_axis + len(places) :]

    @pl.when(pl.program_id(0) == 0)
    def _():
        if places[0] is None:
            columns = pl.ds(start_column, weight.shape[1])
            copies = [pltpu.make_async_copy(weight_refs[0].at[:, columns], weight, sem.at[0])]
        else:
            copies = shard_copies(weight_refs, places, place_ref, heads_axis, rows, start_column, weight, sem)
        for copy in copies:
            copy.start()
        for copy in copies:
            copy.wait()

    count = out_ref.shape[0] * out_ref.shape[1]
    model_width = out_ref.shape[2]

    def half(own_refs):
        total = tokens_ref[...].reshape(count, model_width).astype(jnp.float32)
        for k, ref in enumerate(own_refs):
            width = ref.shape[2]
            start = pl.multiple_of((place_ref[1] ^ k) * width, width)
            total = total + lax.dot_general(
                ref[...].reshape(count, width),
                weight[:, pl.ds(start, width)],
                NT,
                preferred_element_type=jnp.float32,
            )
        normed = normalize(total, gain_ref[0:1, :], shift_ref[0:1, :])
        out_ref[...] = normed.astype(jnp.bfloat16).reshape(out_ref.shape)

    for n in range(halves):
        own_refs = context_refs[n * heads_axis : (n + 1) * heads_axis]
        pl.when(pl.program_id(0) * halves // pl.num_programs(0) == n)(functools.partial(half, own_refs))


def project(place, tokens, contexts, blocks, gain, shift, rows, start_column):
    prompts, seq_len, model_width = tokens.shape
    heads_axis = len(contexts[0])
    row_count, width = contexts[0][0].shape[1:]
    group = max(prompts // 4, 1)
    steps = prompts // group
    share = contexts[0][0].shape[0] // group
    places = [at for _, at in blocks]
    copies = 1 if places[0] is None else sum(len(at) for at in places)
    return pl.pallas_call(
        functools.partial(project_kernel, places, heads_axis, rows, start_column),
        out_shape=jax.ShapeDtypeStruct((prompts, row_count, model_width), jnp.bfloat16),
        grid_spec=pltpu.PrefetchScalarGridSpec(
            num_scalar_prefetch=1,
            grid=(steps,),
            in_specs=[pl.BlockSpec((group, row_count, model_width), lambda p, place: (p, place[1], 0))]
            + [pl.BlockSpec((group, row_count, width), lambda p, place: (lax.rem(p, share), 0, 0))] * (len(contexts) * heads_axis)
            + [pl.BlockSpec(memory_space=pl.ANY)] * len(blocks)
            + [pl.BlockSpec(gain.shape, lambda p, place: (0, 0))] * 2,
            out_specs=pl.BlockSpec((group, row_count, model_width), lambda p, place: (p, 0, 0)),
            scratch_shapes=[
                pltpu.VMEM((model_width, model_width), jnp.bfloat16),
                pltpu.SemaphoreType.DMA((copies,)),
            ],
        ),
        compiler_params=pltpu.CompilerParams(vmem_limit_bytes=40 * MIB),
        cost_estimate=pl.CostEstimate(
            flops=2 * prompts * row_count * model_width * model_width,
            bytes_accessed=8 * prompts * row_count * model_width,
            transcendentals=0,
        ),
        name="project",
    )(place, tokens, *[c for half in contexts for c in half], *[block for block, _ in blocks], gain, shift)


def mlp_kernel(
    order, rows, chunk, lengths_ref, place_ref, normed_ref, whole_ref, gain_ref, shift_ref, out_ref, *scratch
):
    up_weight, down_weight, products, total, sem = scratch
    step = pl.program_id(0)
    parts = pl.num_programs(0) - 1
    hidden_width = whole_ref.shape[1] // 2

    def fetch(kind, n):
        slot = lax.rem(n, 2)
        start = pl.multiple_of(kind * hidden_width + n * chunk, chunk)
        target = (up_weight, down_weight)[kind]
        return [
            pltpu.make_async_copy(
                whole_ref.at[pl.ds(k * rows, rows), pl.ds(start, chunk)],
                target.at[slot, pl.ds(index * rows, rows), :],
                sem.at[kind, slot, k],
            )
            for k, index in enumerate(order)
        ]

    def start(kind, n):
        for copy in fetch(kind, n):
            copy.start()

    def wait(kind, n):
        for copy in fetch(kind, n):
            copy.wait()

    pl.when(step == 0)(lambda: start(0, step))
    pl.when(step + 1 < parts)(lambda: start(0, step + 1))
    pl.when(step < parts)(lambda: start(1, step))
    pl.when(step < parts)(lambda: wait(0, step))
    pl.when(step > 0)(lambda: wait(1, step - 1))

    def up():
        slot = lax.rem(step, 2)
        products[slot] = jnp.dot(normed_ref[...], up_weight[slot], preferred_element_type=jnp.float32)

    def down(at):
        slot = lax.rem(step + 1, 2)
        values = products[slot, at, :]
        hidden = (0.5 * values * (1.0 + lax.erf(values * math.sqrt(0.5)))).astype(jnp.bfloat16)
        return lax.dot_general(hidden, down_weight[slot], NT, preferred_element_type=jnp.float32)

    everything = slice(0, normed_ref.shape[0])

    @pl.when(step == 0)
    def _():
        up()

    @pl.when(step == 1)
    def _():
        up()
        total[...] = down(everything)

    @pl.when((step > 1) & (step < parts))
    def _():
        up()
        total[...] += down(everything)

    @pl.when(step == parts)
    def _():
        prompts, row_count, _ = out_ref.shape
        position = place_ref[1] * row_count + lax.broadcasted_iota(jnp.int32, (row_count, 1), 0)
        pair = 2 if prompts % 2 == 0 else 1
        for p in range(0, prompts, pair):
            at = slice(p * row_count, (p + pair) * row_count)
            summed = normed_ref[at, :].astype(jnp.float32) + total[at, :] + down(at)
            finished = normalize(summed, gain_ref[1:2, :], shift_ref[1:2, :])
            for n in range(pair):
                part = finished[n * row_count : (n + 1) * row_count, :]
                inside = position < lengths_ref[p + n]
                out_ref[p + n] = jnp.where(inside, part, 0.0).astype(jnp.bfloat16)


def mlp(lengths, place, normed, whole, order, rows, gain, shift, prompts, chunk):
    count, model_width = normed.shape
    hidden_width = whole.shape[1] // 2
    row_count = count // prompts
    constant = lambda n, *_: (0, 0)
    return pl.pallas_call(
        functools.partial(mlp_kernel, order, rows, chunk),
        out_shape=jax.ShapeDtypeStruct((prompts, row_count, model_width), jnp.bfloat16),
        grid_spec=pltpu.PrefetchScalarGridSpec(
            num_scalar_prefetch=2,
            grid=(hidden_width // chunk + 1,),
            in_specs=[
                pl.BlockSpec((count, model_width), constant),
                pl.BlockSpec(memory_space=pl.ANY),
                pl.BlockSpec(gain.shape, constant),
                pl.BlockSpec(gain.shape, constant),
            ],
            out_specs=pl.BlockSpec((prompts, row_count, model_width), lambda n, *_: (0, 0, 0)),
            scratch_shapes=[
                pltpu.VMEM((2, model_width, chunk), jnp.bfloat16),
                pltpu.VMEM((2, model_width, chunk), jnp.bfloat16),
                pltpu.VMEM((2, count, chunk), jnp.float32),
                pltpu.VMEM((count, model_width), jnp.float32),
                pltpu.SemaphoreType.DMA((2, 2, len(order))),
            ],
        ),
        compiler_params=pltpu.CompilerParams(vmem_limit_bytes=60 * MIB),
        cost_estimate=pl.CostEstimate(
            flops=4 * count * model_width * hidden_width,
            bytes_accessed=4 * model_width * hidden_width + 6 * count * model_width,
            transcendentals=count * hidden_width,
        ),
        name="mlp",
    )(lengths, place, normed, whole, gain, shift)


def shards(tokens, lengths, attn_in, attn_out, mlp_in, mlp_out, norm_gain, norm_shift):
    heads_axis = lax.axis_size("head")
    prompts, seq_len, model_width = tokens.shape
    hidden_width = mlp_in.shape[1]
    width = model_width // heads_axis
    row_count = seq_len // heads_axis
    rows = mlp_in.shape[0]
    place = jnp.stack([lax.axis_index("seq"), lax.axis_index("head")]).astype(jnp.int32)
    half = hidden_width // 2
    quarter = hidden_width // 4

    def both(start, stop):
        return [mlp_in[:, start:stop], mlp_out.T[:, start:stop]]

    def packed(pieces):
        return jnp.concatenate(pieces, axis=1).astype(jnp.bfloat16)

    in_cast = attn_in.astype(jnp.bfloat16).reshape(rows, 3, heads_axis, width)
    in_cast = in_cast.transpose(2, 0, 1, 3).reshape(heads_axis, rows, 3 * width)
    in_rows = lax.all_to_all(in_cast, "head", 0, 0).reshape(heads_axis * rows, 3 * width)

    whole = gather_cycle(packed(both(0, hidden_width)))
    in_depth = jnp.concatenate(by_depth(in_rows), axis=0)
    out_parts = by_depth(after(attn_out.T.astype(jnp.bfloat16), in_depth))
    in_blocks = [(in_depth, 0), (swap_seq(in_depth, 1), 1)]

    contexts, caches, count = [], [], prompts // ATTENTION_CALLS
    for start in range(0, prompts, count):
        *caches, own, one, two, three = attention(
            lengths, place, tokens, in_blocks, heads_axis, start, count, caches
        )
        contexts.append([own, swap_head(one, 1), swap_head(two, 2), swap_head(three, 3)])
    out_blocks = other_core(across_second(across_first(out_parts)))
    normed = project(place, tokens, contexts, out_blocks, norm_gain, norm_shift, rows, 0)
    normed = normed.reshape(prompts * row_count, model_width)
    whole = after(whole, normed)
    order = [s * heads_axis + h for s, h in cycle()]
    encoded = mlp(lengths, place, normed, whole, order, rows, norm_gain, norm_shift, prompts, hidden_width // 4)
    return (encoded, caches[0], caches[1])


def solution(mesh):
    in_specs = (
        P("seq", None, None),
        P("seq"),
        P(("seq", "head"), None, None),
        P(None, ("seq", "head")),
        P(("seq", "head"), None),
        P(None, ("seq", "head")),
        P(),
        P(),
    )
    out_specs = (P("seq", "head", None), P("seq", None, "head"), P("seq", None, "head"))
    return jax.shard_map(shards, mesh=mesh, in_specs=in_specs, out_specs=out_specs, check_vma=False)
```

```python
import functools
import math

import jax
import jax.numpy as jnp
from jax import lax
from jax.experimental import pallas as pl
from jax.experimental.pallas import tpu as pltpu
from jax.sharding import PartitionSpec as P

DH = 64
EPSILON = 1e-05
TILE = 128
NT = (((1,), (1,)), ((), ()))
MIB = 1024 * 1024
ATTENTION_CALLS = 1


def swap_seq(x, k):
    return lax.ppermute(x, "seq", [(i, i ^ k) for i in range(lax.axis_size("seq"))])


def swap_head(x, k):
    return lax.ppermute(x, "head", [(i, i ^ k) for i in range(lax.axis_size("head"))])


def depths():
    return list(range(0, lax.axis_size("seq"), 2))


def after(x, *done):
    return lax.optimization_barrier((x, done))[0]


def along_depth(x):
    groups = [[d + core for d in depths()] for core in range(2)]
    return lax.all_gather(x, "seq", axis=0, tiled=True, axis_index_groups=groups)


def by_depth(x):
    return [x] + [swap_seq(x, k) for k in depths()[1:]]


def across_first(parts):
    half = len(parts) // 2
    lower, upper = jnp.concatenate(parts[:half], axis=0), jnp.concatenate(parts[half:], axis=0)
    return [[lower, swap_head(lower, 1), swap_head(lower, 2)], [upper, swap_head(upper, 2), swap_head(upper, 1)]]


def across_second(first):
    half = len(depths()) // 2
    blocks = []
    for (own, one, two), (a, b), at in zip(first, ((1, 2), (2, 1)), (depths()[:half], depths()[half:])):
        for block, h in ((own, 0), (one, a), (two, b), (swap_head(one, b), 3)):
            blocks.append((block, [(-1, s, h) for s in at]))
    return blocks


def cycle():
    seq = list(range(lax.axis_size("seq")))
    order = []
    for n in range(len(seq) // 2):
        for h in across_order()[:: 1 if n % 2 == 0 else -1]:
            order.extend([(2 * n, h), (2 * n + 1, h)])
    return order


def across_order():
    return [n ^ (n >> 1) for n in range(lax.axis_size("head"))]


def gather_cycle(x):
    heads = lax.axis_size("head")
    group = [s * heads + h for s, h in cycle()]
    return lax.all_gather(x, ("seq", "head"), axis=0, tiled=True, axis_index_groups=[group])


def other_core(blocks):
    return blocks + [(swap_seq(b, 1), [(m, s ^ 1, h) for m, s, h in at]) for b, at in blocks]


def shard_copies(refs, places, place_ref, heads_axis, rows, start, target, sem):
    copies = []
    for ref, at in zip(refs, places):
        for n, (mask, s, h) in enumerate(at):
            index = s * heads_axis + h if mask is None else (place_ref[0] & mask ^ s) * heads_axis + (place_ref[1] ^ h)
            copies.append(
                pltpu.make_async_copy(
                    ref.at[pl.ds(n * rows, rows), pl.ds(start, target.shape[1])],
                    target.at[pl.ds(index * rows if mask is None else pl.multiple_of(index * rows, rows), rows), :],
                    sem.at[len(copies)],
                )
            )
    return copies


def attention_kernel(places, heads_axis, rows, first, aliases, *refs):
    lengths_ref, place_ref, tokens_ref = refs[:3]
    weight_refs = refs[3 : 3 + len(places)]
    refs = refs[:3] + weight_refs + refs[3 + len(places) + aliases :]
    key_ref, value_ref = refs[3 + len(places) : 5 + len(places)]
    context_refs = refs[5 + len(places) : 5 + len(places) + heads_axis]
    weight, held, sem = refs[5 + len(places) + heads_axis :]
    prompt = pl.program_id(0)
    width = key_ref.shape[2]
    seq_len = key_ref.shape[1]
    row_count = context_refs[0].shape[1]

    @pl.when(prompt == 0)
    def _():
        copies = []
        for core, ref in zip(places, weight_refs):
            for depth in range(ref.shape[0] // rows):
                start = pl.multiple_of((place_ref[0] ^ (2 * depth + core)) * rows, rows)
                copies.append(
                    pltpu.make_async_copy(
                        ref.at[pl.ds(depth * rows, rows), :],
                        weight.at[pl.ds(start, rows), :],
                        sem.at[len(copies)],
                    )
                )
        for copy in copies:
            copy.start()
        for copy in copies:
            copy.wait()

    length = lengths_ref[first + prompt]
    filled = (length + TILE - 1) // TILE
    lanes = lax.broadcasted_iota(jnp.int32, (1, width), 1) // DH

    def part(tiles):
        span = tiles * TILE
        projected = jnp.dot(tokens_ref[0, :span, :], weight[...], preferred_element_type=jnp.float32)
        queries = (projected[:, :width] * (math.log2(math.e) / math.sqrt(DH))).astype(jnp.bfloat16)
        keys = projected[:, width : 2 * width].astype(jnp.bfloat16)
        values = projected[:, 2 * width :].astype(jnp.bfloat16)
        inside = lax.broadcasted_iota(jnp.int32, (span, 1), 0) < length
        key_ref[0, :span, :] = jnp.where(inside, keys, jnp.zeros_like(keys))
        value_ref[0, :span, :] = jnp.where(inside, values, jnp.zeros_like(values))
        if span < seq_len:
            rest = jnp.zeros((seq_len - span, width), jnp.bfloat16)
            key_ref[0, span:, :] = rest
            value_ref[0, span:, :] = rest
            held[span:, :] = rest
        column = lax.broadcasted_iota(jnp.int32, (1, span), 1) < length
        context = jnp.zeros((span, width), jnp.float32)
        for head in range(width // DH):
            mine = lanes == head
            query = jnp.where(mine, queries, jnp.zeros_like(queries))
            scores = lax.dot_general(query, keys, NT, preferred_element_type=jnp.float32)
            scores = jnp.where(column, scores, -1e30)
            raised = jnp.exp2(scores - jnp.max(scores, axis=-1, keepdims=True))
            total = jnp.sum(raised, axis=-1, keepdims=True)
            out = jnp.dot(raised.astype(jnp.bfloat16), values, preferred_element_type=jnp.float32)
            context = jnp.where(mine, out * (1.0 / total), context)
        held[:span, :] = context.astype(jnp.bfloat16)

    for tiles in range(1, seq_len // TILE + 1):
        pl.when(filled == tiles)(functools.partial(part, tiles))
    for k, ref in enumerate(context_refs):
        start = pl.multiple_of((place_ref[1] ^ k) * row_count, row_count)
        ref[0] = held[pl.ds(start, row_count), :]


def attention(lengths, place, tokens, weight_blocks, heads_axis, first, count, caches):
    prompts, seq_len, model_width = tokens.shape
    width = model_width // heads_axis
    row_count = seq_len // heads_axis
    rows = model_width // lax.axis_size("seq")
    cache = jax.ShapeDtypeStruct((prompts, seq_len, width), jnp.bfloat16)
    piece = jax.ShapeDtypeStruct((count, row_count, width), jnp.bfloat16)
    by_prompt = lambda p, *_: (p, 0, 0)
    shifted = lambda p, *_: (first + p, 0, 0)
    return pl.pallas_call(
        functools.partial(attention_kernel, [s for _, s in weight_blocks], heads_axis, rows, first, len(caches)),
        out_shape=[cache, cache] + [piece] * heads_axis,
        grid_spec=pltpu.PrefetchScalarGridSpec(
            num_scalar_prefetch=2,
            grid=(count,),
            in_specs=[pl.BlockSpec((1, seq_len, model_width), shifted)]
            + [pl.BlockSpec(memory_space=pl.ANY)] * (len(weight_blocks) + len(caches)),
            out_specs=[pl.BlockSpec((1, seq_len, width), shifted)] * 2
            + [pl.BlockSpec((1, row_count, width), by_prompt)] * heads_axis,
            scratch_shapes=[
                pltpu.VMEM((model_width, 3 * width), jnp.bfloat16),
                pltpu.VMEM((seq_len, width), jnp.bfloat16),
                pltpu.SemaphoreType.DMA((model_width // rows,)),
            ],
        ),
        input_output_aliases={3 + len(weight_blocks) + n: n for n in range(len(caches))},
        compiler_params=pltpu.CompilerParams(vmem_limit_bytes=62 * MIB),
        cost_estimate=pl.CostEstimate(
            flops=2 * count * seq_len * model_width * 3 * width + 8 * count * seq_len * seq_len * width,
            bytes_accessed=4 * count * seq_len * model_width,
            transcendentals=count * seq_len * seq_len * width // DH,
        ),
        name="attention",
    )(lengths, place, tokens, *[block for block, _ in weight_blocks], *caches)


def normalize(values, gain, shift):
    center = values - jnp.mean(values, axis=-1, keepdims=True)
    spread = jnp.mean(center * center, axis=-1, keepdims=True)
    return center * lax.rsqrt(spread + EPSILON) * gain + shift


def project_kernel(places, heads_axis, rows, start_column, *refs):
    place_ref, tokens_ref = refs[:2]
    halves = (len(refs) - 2 - len(places) - 5) // heads_axis
    context_refs = refs[2 : 2 + halves * heads_axis]
    weight_refs = refs[2 + halves * heads_axis : 2 + halves * heads_axis + len(places)]
    gain_ref, shift_ref, out_ref, weight, sem = refs[2 + halves * heads_axis + len(places) :]

    @pl.when(pl.program_id(0) == 0)
    def _():
        if places[0] is None:
            columns = pl.ds(start_column, weight.shape[1])
            copies = [pltpu.make_async_copy(weight_refs[0].at[:, columns], weight, sem.at[0])]
        else:
            copies = shard_copies(weight_refs, places, place_ref, heads_axis, rows, start_column, weight, sem)
        for copy in copies:
            copy.start()
        for copy in copies:
            copy.wait()

    count = out_ref.shape[0] * out_ref.shape[1]
    model_width = out_ref.shape[2]

    def half(own_refs):
        total = tokens_ref[...].reshape(count, model_width).astype(jnp.float32)
        for k, ref in enumerate(own_refs):
            width = ref.shape[2]
            start = pl.multiple_of((place_ref[1] ^ k) * width, width)
            total = total + lax.dot_general(
                ref[...].reshape(count, width),
                weight[:, pl.ds(start, width)],
                NT,
                preferred_element_type=jnp.float32,
            )
        normed = normalize(total, gain_ref[0:1, :], shift_ref[0:1, :])
        out_ref[...] = normed.astype(jnp.bfloat16).reshape(out_ref.shape)

    for n in range(halves):
        own_refs = context_refs[n * heads_axis : (n + 1) * heads_axis]
        pl.when(pl.program_id(0) * halves // pl.num_programs(0) == n)(functools.partial(half, own_refs))


def project(place, tokens, contexts, blocks, gain, shift, rows, start_column):
    prompts, seq_len, model_width = tokens.shape
    heads_axis = len(contexts[0])
    row_count, width = contexts[0][0].shape[1:]
    group = max(prompts // 4, 1)
    steps = prompts // group
    share = contexts[0][0].shape[0] // group
    places = [at for _, at in blocks]
    copies = 1 if places[0] is None else sum(len(at) for at in places)
    return pl.pallas_call(
        functools.partial(project_kernel, places, heads_axis, rows, start_column),
        out_shape=jax.ShapeDtypeStruct((prompts, row_count, model_width), jnp.bfloat16),
        grid_spec=pltpu.PrefetchScalarGridSpec(
            num_scalar_prefetch=1,
            grid=(steps,),
            in_specs=[pl.BlockSpec((group, row_count, model_width), lambda p, place: (p, place[1], 0))]
            + [pl.BlockSpec((group, row_count, width), lambda p, place: (lax.rem(p, share), 0, 0))] * (len(contexts) * heads_axis)
            + [pl.BlockSpec(memory_space=pl.ANY)] * len(blocks)
            + [pl.BlockSpec(gain.shape, lambda p, place: (0, 0))] * 2,
            out_specs=pl.BlockSpec((group, row_count, model_width), lambda p, place: (p, 0, 0)),
            scratch_shapes=[
                pltpu.VMEM((model_width, model_width), jnp.bfloat16),
                pltpu.SemaphoreType.DMA((copies,)),
            ],
        ),
        compiler_params=pltpu.CompilerParams(vmem_limit_bytes=40 * MIB),
        cost_estimate=pl.CostEstimate(
            flops=2 * prompts * row_count * model_width * model_width,
            bytes_accessed=8 * prompts * row_count * model_width,
            transcendentals=0,
        ),
        name="project",
    )(place, tokens, *[c for half in contexts for c in half], *[block for block, _ in blocks], gain, shift)


def mlp_kernel(
    order, rows, chunk, lengths_ref, place_ref, normed_ref, whole_ref, gain_ref, shift_ref, out_ref, *scratch
):
    up_weight, down_weight, products, total, sem = scratch
    step = pl.program_id(0)
    parts = pl.num_programs(0) - 1
    hidden_width = whole_ref.shape[1] // 2

    def fetch(kind, n):
        slot = lax.rem(n, 2)
        start = pl.multiple_of(kind * hidden_width + n * chunk, chunk)
        target = (up_weight, down_weight)[kind]
        return [
            pltpu.make_async_copy(
                whole_ref.at[pl.ds(k * rows, rows), pl.ds(start, chunk)],
                target.at[slot, pl.ds(index * rows, rows), :],
                sem.at[kind, slot, k],
            )
            for k, index in enumerate(order)
        ]

    def start(kind, n):
        for copy in fetch(kind, n):
            copy.start()

    def wait(kind, n):
        for copy in fetch(kind, n):
            copy.wait()

    pl.when(step == 0)(lambda: start(0, step))
    pl.when(step + 1 < parts)(lambda: start(0, step + 1))
    pl.when(step < parts)(lambda: start(1, step))
    pl.when(step < parts)(lambda: wait(0, step))
    pl.when(step > 0)(lambda: wait(1, step - 1))

    def up():
        slot = lax.rem(step, 2)
        products[slot] = jnp.dot(normed_ref[...], up_weight[slot], preferred_element_type=jnp.float32)

    def down(at):
        slot = lax.rem(step + 1, 2)
        values = products[slot, at, :]
        hidden = (0.5 * values * (1.0 + lax.erf(values * math.sqrt(0.5)))).astype(jnp.bfloat16)
        return lax.dot_general(hidden, down_weight[slot], NT, preferred_element_type=jnp.float32)

    everything = slice(0, normed_ref.shape[0])

    @pl.when(step == 0)
    def _():
        up()

    @pl.when(step == 1)
    def _():
        up()
        total[...] = down(everything)

    @pl.when((step > 1) & (step < parts))
    def _():
        up()
        total[...] += down(everything)

    @pl.when(step == parts)
    def _():
        prompts, row_count, _ = out_ref.shape
        position = place_ref[1] * row_count + lax.broadcasted_iota(jnp.int32, (row_count, 1), 0)
        pair = 2 if prompts % 2 == 0 else 1
        for p in range(0, prompts, pair):
            at = slice(p * row_count, (p + pair) * row_count)
            summed = normed_ref[at, :].astype(jnp.float32) + total[at, :] + down(at)
            finished = normalize(summed, gain_ref[1:2, :], shift_ref[1:2, :])
            for n in range(pair):
                part = finished[n * row_count : (n + 1) * row_count, :]
                inside = position < lengths_ref[p + n]
                out_ref[p + n] = jnp.where(inside, part, 0.0).astype(jnp.bfloat16)


def mlp(lengths, place, normed, whole, order, rows, gain, shift, prompts, chunk):
    count, model_width = normed.shape
    hidden_width = whole.shape[1] // 2
    row_count = count // prompts
    constant = lambda n, *_: (0, 0)
    return pl.pallas_call(
        functools.partial(mlp_kernel, order, rows, chunk),
        out_shape=jax.ShapeDtypeStruct((prompts, row_count, model_width), jnp.bfloat16),
        grid_spec=pltpu.PrefetchScalarGridSpec(
            num_scalar_prefetch=2,
            grid=(hidden_width // chunk + 1,),
            in_specs=[
                pl.BlockSpec((count, model_width), constant),
                pl.BlockSpec(memory_space=pl.ANY),
                pl.BlockSpec(gain.shape, constant),
                pl.BlockSpec(gain.shape, constant),
            ],
            out_specs=pl.BlockSpec((prompts, row_count, model_width), lambda n, *_: (0, 0, 0)),
            scratch_shapes=[
                pltpu.VMEM((2, model_width, chunk), jnp.bfloat16),
                pltpu.VMEM((2, model_width, chunk), jnp.bfloat16),
                pltpu.VMEM((2, count, chunk), jnp.float32),
                pltpu.VMEM((count, model_width), jnp.float32),
                pltpu.SemaphoreType.DMA((2, 2, len(order))),
            ],
        ),
        compiler_params=pltpu.CompilerParams(vmem_limit_bytes=60 * MIB),
        cost_estimate=pl.CostEstimate(
            flops=4 * count * model_width * hidden_width,
            bytes_accessed=4 * model_width * hidden_width + 6 * count * model_width,
            transcendentals=count * hidden_width,
        ),
        name="mlp",
    )(lengths, place, normed, whole, gain, shift)


def shards(tokens, lengths, attn_in, attn_out, mlp_in, mlp_out, norm_gain, norm_shift):
    heads_axis = lax.axis_size("head")
    prompts, seq_len, model_width = tokens.shape
    hidden_width = mlp_in.shape[1]
    width = model_width // heads_axis
    row_count = seq_len // heads_axis
    rows = mlp_in.shape[0]
    place = jnp.stack([lax.axis_index("seq"), lax.axis_index("head")]).astype(jnp.int32)
    half = hidden_width // 2
    quarter = hidden_width // 4

    def both(start, stop):
        return [mlp_in[:, start:stop], mlp_out.T[:, start:stop]]

    def packed(pieces):
        return jnp.concatenate(pieces, axis=1).astype(jnp.bfloat16)

    in_cast = attn_in.astype(jnp.bfloat16).reshape(rows, 3, heads_axis, width)
    in_cast = in_cast.transpose(2, 0, 1, 3).reshape(heads_axis, rows, 3 * width)
    in_rows = lax.all_to_all(in_cast, "head", 0, 0).reshape(heads_axis * rows, 3 * width)

    whole = gather_cycle(packed(both(0, hidden_width)))
    out_parts = by_depth(attn_out.T.astype(jnp.bfloat16))
    in_parts = by_depth(after(in_rows, out_parts))
    in_parts, out_first = lax.optimization_barrier((in_parts, across_first(out_parts)))
    in_depth = jnp.concatenate(in_parts, axis=0)
    in_blocks = [(in_depth, 0), (swap_seq(in_depth, 1), 1)]

    contexts, caches, count = [], [], prompts // ATTENTION_CALLS
    for start in range(0, prompts, count):
        *caches, own, one, two, three = attention(
            lengths, place, tokens, in_blocks, heads_axis, start, count, caches
        )
        contexts.append([own, swap_head(one, 1), swap_head(two, 2), swap_head(three, 3)])
    out_blocks = other_core(across_second(out_first))
    normed = project(place, tokens, contexts, out_blocks, norm_gain, norm_shift, rows, 0)
    normed = normed.reshape(prompts * row_count, model_width)
    whole = after(whole, normed)
    order = [s * heads_axis + h for s, h in cycle()]
    encoded = mlp(lengths, place, normed, whole, order, rows, norm_gain, norm_shift, prompts, hidden_width // 4)
    return (encoded, caches[0], caches[1])


def solution(mesh):
    in_specs = (
        P("seq", None, None),
        P("seq"),
        P(("seq", "head"), None, None),
        P(None, ("seq", "head")),
        P(("seq", "head"), None),
        P(None, ("seq", "head")),
        P(),
        P(),
    )
    out_specs = (P("seq", "head", None), P("seq", None, "head"), P("seq", None, "head"))
    return jax.shard_map(shards, mesh=mesh, in_specs=in_specs, out_specs=out_specs, check_vma=False)
```

```python
import functools
import math

import jax
import jax.numpy as jnp
from jax import lax
from jax.experimental import pallas as pl
from jax.experimental.pallas import tpu as pltpu
from jax.sharding import PartitionSpec as P

DH = 64
EPSILON = 1e-05
TILE = 128
NT = (((1,), (1,)), ((), ()))
MIB = 1024 * 1024
ATTENTION_CALLS = 1


def swap_seq(x, k):
    return lax.ppermute(x, "seq", [(i, i ^ k) for i in range(lax.axis_size("seq"))])


def swap_head(x, k):
    return lax.ppermute(x, "head", [(i, i ^ k) for i in range(lax.axis_size("head"))])


def depths():
    return list(range(0, lax.axis_size("seq"), 2))


def after(x, *done):
    return lax.optimization_barrier((x, done))[0]


def by_depth(x):
    return [x] + [swap_seq(x, k) for k in depths()[1:]]


def across_first(parts):
    half = len(parts) // 2
    lower, upper = jnp.concatenate(parts[:half], axis=0), jnp.concatenate(parts[half:], axis=0)
    return [[lower, swap_head(lower, 1), swap_head(lower, 2)], [upper, swap_head(upper, 2), swap_head(upper, 1)]]


def across_second(first):
    half = len(depths()) // 2
    blocks = []
    for (own, one, two), (a, b), at in zip(first, ((1, 2), (2, 1)), (depths()[:half], depths()[half:])):
        for block, h in ((own, 0), (one, a), (two, b), (swap_head(one, b), 3)):
            blocks.append((block, [(-1, s, h) for s in at]))
    return blocks


def cycle():
    seq = list(range(lax.axis_size("seq")))
    order = []
    for n in range(len(seq) // 2):
        for h in across_order()[:: 1 if n % 2 == 0 else -1]:
            order.extend([(2 * n, h), (2 * n + 1, h)])
    return order


def across_order():
    return [n ^ (n >> 1) for n in range(lax.axis_size("head"))]


def gather_cycle(x):
    heads = lax.axis_size("head")
    group = [s * heads + h for s, h in cycle()]
    return lax.all_gather(x, ("seq", "head"), axis=0, tiled=True, axis_index_groups=[group])


def other_core(blocks):
    return blocks + [(swap_seq(b, 1), [(m, s ^ 1, h) for m, s, h in at]) for b, at in blocks]


def shard_copies(refs, places, place_ref, heads_axis, rows, start, target, sem):
    copies = []
    for ref, at in zip(refs, places):
        for n, (mask, s, h) in enumerate(at):
            index = s * heads_axis + h if mask is None else (place_ref[0] & mask ^ s) * heads_axis + (place_ref[1] ^ h)
            copies.append(
                pltpu.make_async_copy(
                    ref.at[pl.ds(n * rows, rows), pl.ds(start, target.shape[1])],
                    target.at[pl.ds(index * rows if mask is None else pl.multiple_of(index * rows, rows), rows), :],
                    sem.at[len(copies)],
                )
            )
    return copies


def attention_kernel(places, heads_axis, rows, first, aliases, *refs):
    lengths_ref, place_ref, tokens_ref = refs[:3]
    weight_refs = refs[3 : 3 + len(places)]
    refs = refs[:3] + weight_refs + refs[3 + len(places) + aliases :]
    key_ref, value_ref = refs[3 + len(places) : 5 + len(places)]
    context_refs = refs[5 + len(places) : 5 + len(places) + heads_axis]
    weight, held, sem = refs[5 + len(places) + heads_axis :]
    prompt = pl.program_id(0)
    width = key_ref.shape[2]
    seq_len = key_ref.shape[1]
    row_count = context_refs[0].shape[1]

    @pl.when(prompt == 0)
    def _():
        copies = []
        for core, ref in zip(places, weight_refs):
            for depth in range(ref.shape[0] // rows):
                start = pl.multiple_of((place_ref[0] ^ (2 * depth + core)) * rows, rows)
                copies.append(
                    pltpu.make_async_copy(
                        ref.at[pl.ds(depth * rows, rows), :],
                        weight.at[pl.ds(start, rows), :],
                        sem.at[len(copies)],
                    )
                )
        for copy in copies:
            copy.start()
        for copy in copies:
            copy.wait()

    length = lengths_ref[first + prompt]
    filled = (length + TILE - 1) // TILE
    lanes = lax.broadcasted_iota(jnp.int32, (1, width), 1) // DH

    def part(tiles):
        span = tiles * TILE
        projected = jnp.dot(tokens_ref[0, :span, :], weight[...], preferred_element_type=jnp.float32)
        queries = (projected[:, :width] * (math.log2(math.e) / math.sqrt(DH))).astype(jnp.bfloat16)
        keys = projected[:, width : 2 * width].astype(jnp.bfloat16)
        values = projected[:, 2 * width :].astype(jnp.bfloat16)
        inside = lax.broadcasted_iota(jnp.int32, (span, 1), 0) < length
        key_ref[0, :span, :] = jnp.where(inside, keys, jnp.zeros_like(keys))
        value_ref[0, :span, :] = jnp.where(inside, values, jnp.zeros_like(values))
        if span < seq_len:
            rest = jnp.zeros((seq_len - span, width), jnp.bfloat16)
            key_ref[0, span:, :] = rest
            value_ref[0, span:, :] = rest
            held[span:, :] = rest
        column = lax.broadcasted_iota(jnp.int32, (1, span), 1) < length
        context = jnp.zeros((span, width), jnp.float32)
        for head in range(width // DH):
            mine = lanes == head
            query = jnp.where(mine, queries, jnp.zeros_like(queries))
            scores = lax.dot_general(query, keys, NT, preferred_element_type=jnp.float32)
            scores = jnp.where(column, scores, -1e30)
            raised = jnp.exp2(scores - jnp.max(scores, axis=-1, keepdims=True))
            total = jnp.sum(raised, axis=-1, keepdims=True)
            out = jnp.dot(raised.astype(jnp.bfloat16), values, preferred_element_type=jnp.float32)
            context = jnp.where(mine, out * (1.0 / total), context)
        held[:span, :] = context.astype(jnp.bfloat16)

    for tiles in range(1, seq_len // TILE + 1):
        pl.when(filled == tiles)(functools.partial(part, tiles))
    for k, ref in enumerate(context_refs):
        start = pl.multiple_of((place_ref[1] ^ k) * row_count, row_count)
        ref[0] = held[pl.ds(start, row_count), :]


def attention(lengths, place, tokens, weight_blocks, heads_axis, first, count, caches):
    prompts, seq_len, model_width = tokens.shape
    width = model_width // heads_axis
    row_count = seq_len // heads_axis
    rows = model_width // lax.axis_size("seq")
    cache = jax.ShapeDtypeStruct((prompts, seq_len, width), jnp.bfloat16)
    piece = jax.ShapeDtypeStruct((count, row_count, width), jnp.bfloat16)
    by_prompt = lambda p, *_: (p, 0, 0)
    shifted = lambda p, *_: (first + p, 0, 0)
    return pl.pallas_call(
        functools.partial(attention_kernel, [s for _, s in weight_blocks], heads_axis, rows, first, len(caches)),
        out_shape=[cache, cache] + [piece] * heads_axis,
        grid_spec=pltpu.PrefetchScalarGridSpec(
            num_scalar_prefetch=2,
            grid=(count,),
            in_specs=[pl.BlockSpec((1, seq_len, model_width), shifted)]
            + [pl.BlockSpec(memory_space=pl.ANY)] * (len(weight_blocks) + len(caches)),
            out_specs=[pl.BlockSpec((1, seq_len, width), shifted)] * 2
            + [pl.BlockSpec((1, row_count, width), by_prompt)] * heads_axis,
            scratch_shapes=[
                pltpu.VMEM((model_width, 3 * width), jnp.bfloat16),
                pltpu.VMEM((seq_len, width), jnp.bfloat16),
                pltpu.SemaphoreType.DMA((model_width // rows,)),
            ],
        ),
        input_output_aliases={3 + len(weight_blocks) + n: n for n in range(len(caches))},
        compiler_params=pltpu.CompilerParams(vmem_limit_bytes=62 * MIB),
        cost_estimate=pl.CostEstimate(
            flops=2 * count * seq_len * model_width * 3 * width + 8 * count * seq_len * seq_len * width,
            bytes_accessed=4 * count * seq_len * model_width,
            transcendentals=count * seq_len * seq_len * width // DH,
        ),
        name="attention",
    )(lengths, place, tokens, *[block for block, _ in weight_blocks], *caches)


def normalize(values, gain, shift):
    center = values - jnp.mean(values, axis=-1, keepdims=True)
    spread = jnp.mean(center * center, axis=-1, keepdims=True)
    return center * lax.rsqrt(spread + EPSILON) * gain + shift


def project_kernel(places, heads_axis, rows, start_column, *refs):
    place_ref, tokens_ref = refs[:2]
    halves = (len(refs) - 2 - len(places) - 5) // heads_axis
    context_refs = refs[2 : 2 + halves * heads_axis]
    weight_refs = refs[2 + halves * heads_axis : 2 + halves * heads_axis + len(places)]
    gain_ref, shift_ref, out_ref, weight, sem = refs[2 + halves * heads_axis + len(places) :]

    @pl.when(pl.program_id(0) == 0)
    def _():
        if places[0] is None:
            columns = pl.ds(start_column, weight.shape[1])
            copies = [pltpu.make_async_copy(weight_refs[0].at[:, columns], weight, sem.at[0])]
        else:
            copies = shard_copies(weight_refs, places, place_ref, heads_axis, rows, start_column, weight, sem)
        for copy in copies:
            copy.start()
        for copy in copies:
            copy.wait()

    count = out_ref.shape[0] * out_ref.shape[1]
    model_width = out_ref.shape[2]

    def half(own_refs):
        total = tokens_ref[...].reshape(count, model_width).astype(jnp.float32)
        for k, ref in enumerate(own_refs):
            width = ref.shape[2]
            start = pl.multiple_of((place_ref[1] ^ k) * width, width)
            total = total + lax.dot_general(
                ref[...].reshape(count, width),
                weight[:, pl.ds(start, width)],
                NT,
                preferred_element_type=jnp.float32,
            )
        normed = normalize(total, gain_ref[0:1, :], shift_ref[0:1, :])
        out_ref[...] = normed.astype(jnp.bfloat16).reshape(out_ref.shape)

    for n in range(halves):
        own_refs = context_refs[n * heads_axis : (n + 1) * heads_axis]
        pl.when(pl.program_id(0) * halves // pl.num_programs(0) == n)(functools.partial(half, own_refs))


def project(place, tokens, contexts, blocks, gain, shift, rows, start_column):
    prompts, seq_len, model_width = tokens.shape
    heads_axis = len(contexts[0])
    row_count, width = contexts[0][0].shape[1:]
    group = max(prompts // 4, 1)
    steps = prompts // group
    share = contexts[0][0].shape[0] // group
    places = [at for _, at in blocks]
    copies = 1 if places[0] is None else sum(len(at) for at in places)
    return pl.pallas_call(
        functools.partial(project_kernel, places, heads_axis, rows, start_column),
        out_shape=jax.ShapeDtypeStruct((prompts, row_count, model_width), jnp.bfloat16),
        grid_spec=pltpu.PrefetchScalarGridSpec(
            num_scalar_prefetch=1,
            grid=(steps,),
            in_specs=[pl.BlockSpec((group, row_count, model_width), lambda p, place: (p, place[1], 0))]
            + [pl.BlockSpec((group, row_count, width), lambda p, place: (lax.rem(p, share), 0, 0))] * (len(contexts) * heads_axis)
            + [pl.BlockSpec(memory_space=pl.ANY)] * len(blocks)
            + [pl.BlockSpec(gain.shape, lambda p, place: (0, 0))] * 2,
            out_specs=pl.BlockSpec((group, row_count, model_width), lambda p, place: (p, 0, 0)),
            scratch_shapes=[
                pltpu.VMEM((model_width, model_width), jnp.bfloat16),
                pltpu.SemaphoreType.DMA((copies,)),
            ],
        ),
        compiler_params=pltpu.CompilerParams(vmem_limit_bytes=40 * MIB),
        cost_estimate=pl.CostEstimate(
            flops=2 * prompts * row_count * model_width * model_width,
            bytes_accessed=8 * prompts * row_count * model_width,
            transcendentals=0,
        ),
        name="project",
    )(place, tokens, *[c for half in contexts for c in half], *[block for block, _ in blocks], gain, shift)


def mlp_kernel(
    order, rows, chunk, lengths_ref, place_ref, normed_ref, whole_ref, gain_ref, shift_ref, out_ref, *scratch
):
    up_weight, down_weight, products, total, sem = scratch
    step = pl.program_id(0)
    parts = pl.num_programs(0) - 1
    hidden_width = whole_ref.shape[1] // 2

    def fetch(kind, n):
        slot = lax.rem(n, 2)
        start = pl.multiple_of(kind * hidden_width + n * chunk, chunk)
        target = (up_weight, down_weight)[kind]
        return [
            pltpu.make_async_copy(
                whole_ref.at[pl.ds(k * rows, rows), pl.ds(start, chunk)],
                target.at[slot, pl.ds(index * rows, rows), :],
                sem.at[kind, slot, k],
            )
            for k, index in enumerate(order)
        ]

    def start(kind, n):
        for copy in fetch(kind, n):
            copy.start()

    def wait(kind, n):
        for copy in fetch(kind, n):
            copy.wait()

    pl.when(step == 0)(lambda: start(0, step))
    pl.when(step + 1 < parts)(lambda: start(0, step + 1))
    pl.when(step < parts)(lambda: start(1, step))
    pl.when(step < parts)(lambda: wait(0, step))
    pl.when(step > 0)(lambda: wait(1, step - 1))

    def up():
        slot = lax.rem(step, 2)
        products[slot] = jnp.dot(normed_ref[...], up_weight[slot], preferred_element_type=jnp.float32)

    def down(at):
        slot = lax.rem(step + 1, 2)
        values = products[slot, at, :]
        hidden = (0.5 * values * (1.0 + lax.erf(values * math.sqrt(0.5)))).astype(jnp.bfloat16)
        return lax.dot_general(hidden, down_weight[slot], NT, preferred_element_type=jnp.float32)

    everything = slice(0, normed_ref.shape[0])

    @pl.when(step == 0)
    def _():
        up()

    @pl.when(step == 1)
    def _():
        up()
        total[...] = down(everything)

    @pl.when((step > 1) & (step < parts))
    def _():
        up()
        total[...] += down(everything)

    @pl.when(step == parts)
    def _():
        prompts, row_count, _ = out_ref.shape
        position = place_ref[1] * row_count + lax.broadcasted_iota(jnp.int32, (row_count, 1), 0)
        pair = 2 if prompts % 2 == 0 else 1
        for p in range(0, prompts, pair):
            at = slice(p * row_count, (p + pair) * row_count)
            summed = normed_ref[at, :].astype(jnp.float32) + total[at, :] + down(at)
            finished = normalize(summed, gain_ref[1:2, :], shift_ref[1:2, :])
            for n in range(pair):
                part = finished[n * row_count : (n + 1) * row_count, :]
                inside = position < lengths_ref[p + n]
                out_ref[p + n] = jnp.where(inside, part, 0.0).astype(jnp.bfloat16)


def mlp(lengths, place, normed, whole, order, rows, gain, shift, prompts, chunk):
    count, model_width = normed.shape
    hidden_width = whole.shape[1] // 2
    row_count = count // prompts
    constant = lambda n, *_: (0, 0)
    return pl.pallas_call(
        functools.partial(mlp_kernel, order, rows, chunk),
        out_shape=jax.ShapeDtypeStruct((prompts, row_count, model_width), jnp.bfloat16),
        grid_spec=pltpu.PrefetchScalarGridSpec(
            num_scalar_prefetch=2,
            grid=(hidden_width // chunk + 1,),
            in_specs=[
                pl.BlockSpec((count, model_width), constant),
                pl.BlockSpec(memory_space=pl.ANY),
                pl.BlockSpec(gain.shape, constant),
                pl.BlockSpec(gain.shape, constant),
            ],
            out_specs=pl.BlockSpec((prompts, row_count, model_width), lambda n, *_: (0, 0, 0)),
            scratch_shapes=[
                pltpu.VMEM((2, model_width, chunk), jnp.bfloat16),
                pltpu.VMEM((2, model_width, chunk), jnp.bfloat16),
                pltpu.VMEM((2, count, chunk), jnp.float32),
                pltpu.VMEM((count, model_width), jnp.float32),
                pltpu.SemaphoreType.DMA((2, 2, len(order))),
            ],
        ),
        compiler_params=pltpu.CompilerParams(vmem_limit_bytes=60 * MIB),
        cost_estimate=pl.CostEstimate(
            flops=4 * count * model_width * hidden_width,
            bytes_accessed=4 * model_width * hidden_width + 6 * count * model_width,
            transcendentals=count * hidden_width,
        ),
        name="mlp",
    )(lengths, place, normed, whole, gain, shift)


def shards(tokens, lengths, attn_in, attn_out, mlp_in, mlp_out, norm_gain, norm_shift):
    heads_axis = lax.axis_size("head")
    prompts, seq_len, model_width = tokens.shape
    hidden_width = mlp_in.shape[1]
    width = model_width // heads_axis
    row_count = seq_len // heads_axis
    rows = mlp_in.shape[0]
    place = jnp.stack([lax.axis_index("seq"), lax.axis_index("head")]).astype(jnp.int32)

    def both(start, stop):
        return [mlp_in[:, start:stop], mlp_out.T[:, start:stop]]

    def packed(pieces):
        return jnp.concatenate(pieces, axis=1).astype(jnp.bfloat16)

    in_cast = attn_in.astype(jnp.bfloat16).reshape(rows, 3, heads_axis, width)
    in_cast = in_cast.transpose(2, 0, 1, 3).reshape(heads_axis, rows, 3 * width)
    in_rows = lax.all_to_all(in_cast, "head", 0, 0).reshape(heads_axis * rows, 3 * width)

    whole = gather_cycle(packed(both(0, hidden_width)))
    out_parts = by_depth(attn_out.T.astype(jnp.bfloat16))
    in_parts = by_depth(after(in_rows, out_parts))
    out_blocks = across_second(across_first(out_parts))
    in_parts, arrived = lax.optimization_barrier((in_parts, [block for block, _ in out_blocks]))
    out_blocks = [(block, at) for block, (_, at) in zip(arrived, out_blocks)]
    in_depth = jnp.concatenate(in_parts, axis=0)
    in_blocks = [(in_depth, 0), (swap_seq(in_depth, 1), 1)]

    contexts, caches, count = [], [], prompts // ATTENTION_CALLS
    for start in range(0, prompts, count):
        *caches, own, one, two, three = attention(
            lengths, place, tokens, in_blocks, heads_axis, start, count, caches
        )
        contexts.append([own, swap_head(one, 1), swap_head(two, 2), swap_head(three, 3)])
    out_blocks = other_core(out_blocks)
    normed = project(place, tokens, contexts, out_blocks, norm_gain, norm_shift, rows, 0)
    normed = normed.reshape(prompts * row_count, model_width)
    whole = after(whole, normed)
    order = [s * heads_axis + h for s, h in cycle()]
    encoded = mlp(lengths, place, normed, whole, order, rows, norm_gain, norm_shift, prompts, hidden_width // 4)
    return (encoded, caches[0], caches[1])


def solution(mesh):
    in_specs = (
        P("seq", None, None),
        P("seq"),
        P(("seq", "head"), None, None),
        P(None, ("seq", "head")),
        P(("seq", "head"), None),
        P(None, ("seq", "head")),
        P(),
        P(),
    )
    out_specs = (P("seq", "head", None), P("seq", None, "head"), P("seq", None, "head"))
    return jax.shard_map(shards, mesh=mesh, in_specs=in_specs, out_specs=out_specs, check_vma=False)
```

```python
import functools
import math

import jax
import jax.numpy as jnp
from jax import lax
from jax.experimental import pallas as pl
from jax.experimental.pallas import tpu as pltpu
from jax.sharding import PartitionSpec as P

DH = 64
EPSILON = 1e-05
TILE = 128
NT = (((1,), (1,)), ((), ()))
MIB = 1024 * 1024
ATTENTION_CALLS = 1


def swap_seq(x, k):
    return lax.ppermute(x, "seq", [(i, i ^ k) for i in range(lax.axis_size("seq"))])


def swap_head(x, k):
    return lax.ppermute(x, "head", [(i, i ^ k) for i in range(lax.axis_size("head"))])


def depths():
    return list(range(0, lax.axis_size("seq"), 2))


def after(x, *done):
    return lax.optimization_barrier((x, done))[0]


def by_depth(x):
    return [x] + [swap_seq(x, k) for k in depths()[1:]]


def across_first(parts):
    half = len(parts) // 2
    lower, upper = jnp.concatenate(parts[:half], axis=0), jnp.concatenate(parts[half:], axis=0)
    return [[lower, swap_head(lower, 1), swap_head(lower, 2)], [upper, swap_head(upper, 2), swap_head(upper, 1)]]


def across_second(first):
    half = len(depths()) // 2
    blocks = []
    for (own, one, two), (a, b), at in zip(first, ((1, 2), (2, 1)), (depths()[:half], depths()[half:])):
        for block, h in ((own, 0), (one, a), (two, b), (swap_head(one, b), 3)):
            blocks.append((block, [(-1, s, h) for s in at]))
    return blocks


def cycle():
    heads = across_order()
    levels = depths()
    chips = [(d, heads[0]) for d in levels]
    for n, d in enumerate(levels[::-1]):
        chips.extend((d, h) for h in (heads[1:] if n % 2 == 0 else heads[:0:-1]))
    return [(d + core, h) for d, h in chips for core in range(2)]


def across_order():
    return [n ^ (n >> 1) for n in range(lax.axis_size("head"))]


def gather_cycle(x):
    heads = lax.axis_size("head")
    group = [s * heads + h for s, h in cycle()]
    return lax.all_gather(x, ("seq", "head"), axis=0, tiled=True, axis_index_groups=[group])


def other_core(blocks):
    return blocks + [(swap_seq(b, 1), [(m, s ^ 1, h) for m, s, h in at]) for b, at in blocks]


def shard_copies(refs, places, place_ref, heads_axis, rows, start, target, sem):
    copies = []
    for ref, at in zip(refs, places):
        for n, (mask, s, h) in enumerate(at):
            index = s * heads_axis + h if mask is None else (place_ref[0] & mask ^ s) * heads_axis + (place_ref[1] ^ h)
            copies.append(
                pltpu.make_async_copy(
                    ref.at[pl.ds(n * rows, rows), pl.ds(start, target.shape[1])],
                    target.at[pl.ds(index * rows if mask is None else pl.multiple_of(index * rows, rows), rows), :],
                    sem.at[len(copies)],
                )
            )
    return copies


def attention_kernel(places, heads_axis, rows, first, aliases, *refs):
    lengths_ref, place_ref, tokens_ref = refs[:3]
    weight_refs = refs[3 : 3 + len(places)]
    refs = refs[:3] + weight_refs + refs[3 + len(places) + aliases :]
    key_ref, value_ref = refs[3 + len(places) : 5 + len(places)]
    context_refs = refs[5 + len(places) : 5 + len(places) + heads_axis]
    weight, held, sem = refs[5 + len(places) + heads_axis :]
    prompt = pl.program_id(0)
    width = key_ref.shape[2]
    seq_len = key_ref.shape[1]
    row_count = context_refs[0].shape[1]

    @pl.when(prompt == 0)
    def _():
        copies = []
        for core, ref in zip(places, weight_refs):
            for depth in range(ref.shape[0] // rows):
                start = pl.multiple_of((place_ref[0] ^ (2 * depth + core)) * rows, rows)
                copies.append(
                    pltpu.make_async_copy(
                        ref.at[pl.ds(depth * rows, rows), :],
                        weight.at[pl.ds(start, rows), :],
                        sem.at[len(copies)],
                    )
                )
        for copy in copies:
            copy.start()
        for copy in copies:
            copy.wait()

    length = lengths_ref[first + prompt]
    filled = (length + TILE - 1) // TILE
    lanes = lax.broadcasted_iota(jnp.int32, (1, width), 1) // DH

    def part(tiles):
        span = tiles * TILE
        projected = jnp.dot(tokens_ref[0, :span, :], weight[...], preferred_element_type=jnp.float32)
        queries = (projected[:, :width] * (math.log2(math.e) / math.sqrt(DH))).astype(jnp.bfloat16)
        keys = projected[:, width : 2 * width].astype(jnp.bfloat16)
        values = projected[:, 2 * width :].astype(jnp.bfloat16)
        inside = lax.broadcasted_iota(jnp.int32, (span, 1), 0) < length
        key_ref[0, :span, :] = jnp.where(inside, keys, jnp.zeros_like(keys))
        value_ref[0, :span, :] = jnp.where(inside, values, jnp.zeros_like(values))
        if span < seq_len:
            rest = jnp.zeros((seq_len - span, width), jnp.bfloat16)
            key_ref[0, span:, :] = rest
            value_ref[0, span:, :] = rest
            held[span:, :] = rest
        column = lax.broadcasted_iota(jnp.int32, (1, span), 1) < length
        context = jnp.zeros((span, width), jnp.float32)
        for head in range(width // DH):
            mine = lanes == head
            query = jnp.where(mine, queries, jnp.zeros_like(queries))
            scores = lax.dot_general(query, keys, NT, preferred_element_type=jnp.float32)
            scores = jnp.where(column, scores, -1e30)
            raised = jnp.exp2(scores - jnp.max(scores, axis=-1, keepdims=True))
            total = jnp.sum(raised, axis=-1, keepdims=True)
            out = jnp.dot(raised.astype(jnp.bfloat16), values, preferred_element_type=jnp.float32)
            context = jnp.where(mine, out * (1.0 / total), context)
        held[:span, :] = context.astype(jnp.bfloat16)

    for tiles in range(1, seq_len // TILE + 1):
        pl.when(filled == tiles)(functools.partial(part, tiles))
    for k, ref in enumerate(context_refs):
        start = pl.multiple_of((place_ref[1] ^ k) * row_count, row_count)
        ref[0] = held[pl.ds(start, row_count), :]


def attention(lengths, place, tokens, weight_blocks, heads_axis, first, count, caches):
    prompts, seq_len, model_width = tokens.shape
    width = model_width // heads_axis
    row_count = seq_len // heads_axis
    rows = model_width // lax.axis_size("seq")
    cache = jax.ShapeDtypeStruct((prompts, seq_len, width), jnp.bfloat16)
    piece = jax.ShapeDtypeStruct((count, row_count, width), jnp.bfloat16)
    by_prompt = lambda p, *_: (p, 0, 0)
    shifted = lambda p, *_: (first + p, 0, 0)
    return pl.pallas_call(
        functools.partial(attention_kernel, [s for _, s in weight_blocks], heads_axis, rows, first, len(caches)),
        out_shape=[cache, cache] + [piece] * heads_axis,
        grid_spec=pltpu.PrefetchScalarGridSpec(
            num_scalar_prefetch=2,
            grid=(count,),
            in_specs=[pl.BlockSpec((1, seq_len, model_width), shifted)]
            + [pl.BlockSpec(memory_space=pl.ANY)] * (len(weight_blocks) + len(caches)),
            out_specs=[pl.BlockSpec((1, seq_len, width), shifted)] * 2
            + [pl.BlockSpec((1, row_count, width), by_prompt)] * heads_axis,
            scratch_shapes=[
                pltpu.VMEM((model_width, 3 * width), jnp.bfloat16),
                pltpu.VMEM((seq_len, width), jnp.bfloat16),
                pltpu.SemaphoreType.DMA((model_width // rows,)),
            ],
        ),
        input_output_aliases={3 + len(weight_blocks) + n: n for n in range(len(caches))},
        compiler_params=pltpu.CompilerParams(vmem_limit_bytes=62 * MIB),
        cost_estimate=pl.CostEstimate(
            flops=2 * count * seq_len * model_width * 3 * width + 8 * count * seq_len * seq_len * width,
            bytes_accessed=4 * count * seq_len * model_width,
            transcendentals=count * seq_len * seq_len * width // DH,
        ),
        name="attention",
    )(lengths, place, tokens, *[block for block, _ in weight_blocks], *caches)


def normalize(values, gain, shift):
    center = values - jnp.mean(values, axis=-1, keepdims=True)
    spread = jnp.mean(center * center, axis=-1, keepdims=True)
    return center * lax.rsqrt(spread + EPSILON) * gain + shift


def project_kernel(places, heads_axis, rows, start_column, *refs):
    place_ref, tokens_ref = refs[:2]
    halves = (len(refs) - 2 - len(places) - 5) // heads_axis
    context_refs = refs[2 : 2 + halves * heads_axis]
    weight_refs = refs[2 + halves * heads_axis : 2 + halves * heads_axis + len(places)]
    gain_ref, shift_ref, out_ref, weight, sem = refs[2 + halves * heads_axis + len(places) :]

    @pl.when(pl.program_id(0) == 0)
    def _():
        if places[0] is None:
            columns = pl.ds(start_column, weight.shape[1])
            copies = [pltpu.make_async_copy(weight_refs[0].at[:, columns], weight, sem.at[0])]
        else:
            copies = shard_copies(weight_refs, places, place_ref, heads_axis, rows, start_column, weight, sem)
        for copy in copies:
            copy.start()
        for copy in copies:
            copy.wait()

    count = out_ref.shape[0] * out_ref.shape[1]
    model_width = out_ref.shape[2]

    def half(own_refs):
        total = tokens_ref[...].reshape(count, model_width).astype(jnp.float32)
        for k, ref in enumerate(own_refs):
            width = ref.shape[2]
            start = pl.multiple_of((place_ref[1] ^ k) * width, width)
            total = total + lax.dot_general(
                ref[...].reshape(count, width),
                weight[:, pl.ds(start, width)],
                NT,
                preferred_element_type=jnp.float32,
            )
        normed = normalize(total, gain_ref[0:1, :], shift_ref[0:1, :])
        out_ref[...] = normed.astype(jnp.bfloat16).reshape(out_ref.shape)

    for n in range(halves):
        own_refs = context_refs[n * heads_axis : (n + 1) * heads_axis]
        pl.when(pl.program_id(0) * halves // pl.num_programs(0) == n)(functools.partial(half, own_refs))


def project(place, tokens, contexts, blocks, gain, shift, rows, start_column):
    prompts, seq_len, model_width = tokens.shape
    heads_axis = len(contexts[0])
    row_count, width = contexts[0][0].shape[1:]
    group = max(prompts // 4, 1)
    steps = prompts // group
    share = contexts[0][0].shape[0] // group
    places = [at for _, at in blocks]
    copies = 1 if places[0] is None else sum(len(at) for at in places)
    return pl.pallas_call(
        functools.partial(project_kernel, places, heads_axis, rows, start_column),
        out_shape=jax.ShapeDtypeStruct((prompts, row_count, model_width), jnp.bfloat16),
        grid_spec=pltpu.PrefetchScalarGridSpec(
            num_scalar_prefetch=1,
            grid=(steps,),
            in_specs=[pl.BlockSpec((group, row_count, model_width), lambda p, place: (p, place[1], 0))]
            + [pl.BlockSpec((group, row_count, width), lambda p, place: (lax.rem(p, share), 0, 0))] * (len(contexts) * heads_axis)
            + [pl.BlockSpec(memory_space=pl.ANY)] * len(blocks)
            + [pl.BlockSpec(gain.shape, lambda p, place: (0, 0))] * 2,
            out_specs=pl.BlockSpec((group, row_count, model_width), lambda p, place: (p, 0, 0)),
            scratch_shapes=[
                pltpu.VMEM((model_width, model_width), jnp.bfloat16),
                pltpu.SemaphoreType.DMA((copies,)),
            ],
        ),
        compiler_params=pltpu.CompilerParams(vmem_limit_bytes=40 * MIB),
        cost_estimate=pl.CostEstimate(
            flops=2 * prompts * row_count * model_width * model_width,
            bytes_accessed=8 * prompts * row_count * model_width,
            transcendentals=0,
        ),
        name="project",
    )(place, tokens, *[c for half in contexts for c in half], *[block for block, _ in blocks], gain, shift)


def mlp_kernel(
    order, rows, chunk, lengths_ref, place_ref, normed_ref, whole_ref, gain_ref, shift_ref, out_ref, *scratch
):
    up_weight, down_weight, products, total, sem = scratch
    step = pl.program_id(0)
    parts = pl.num_programs(0) - 1
    hidden_width = whole_ref.shape[1] // 2

    def fetch(kind, n):
        slot = lax.rem(n, 2)
        start = pl.multiple_of(kind * hidden_width + n * chunk, chunk)
        target = (up_weight, down_weight)[kind]
        return [
            pltpu.make_async_copy(
                whole_ref.at[pl.ds(k * rows, rows), pl.ds(start, chunk)],
                target.at[slot, pl.ds(index * rows, rows), :],
                sem.at[kind, slot, k],
            )
            for k, index in enumerate(order)
        ]

    def start(kind, n):
        for copy in fetch(kind, n):
            copy.start()

    def wait(kind, n):
        for copy in fetch(kind, n):
            copy.wait()

    pl.when(step == 0)(lambda: start(0, step))
    pl.when(step + 1 < parts)(lambda: start(0, step + 1))
    pl.when(step < parts)(lambda: start(1, step))
    pl.when(step < parts)(lambda: wait(0, step))
    pl.when(step > 0)(lambda: wait(1, step - 1))

    def up():
        slot = lax.rem(step, 2)
        products[slot] = jnp.dot(normed_ref[...], up_weight[slot], preferred_element_type=jnp.float32)

    def down(at):
        slot = lax.rem(step + 1, 2)
        values = products[slot, at, :]
        hidden = (0.5 * values * (1.0 + lax.erf(values * math.sqrt(0.5)))).astype(jnp.bfloat16)
        return lax.dot_general(hidden, down_weight[slot], NT, preferred_element_type=jnp.float32)

    everything = slice(0, normed_ref.shape[0])

    @pl.when(step == 0)
    def _():
        up()

    @pl.when(step == 1)
    def _():
        up()
        total[...] = down(everything)

    @pl.when((step > 1) & (step < parts))
    def _():
        up()
        total[...] += down(everything)

    @pl.when(step == parts)
    def _():
        prompts, row_count, _ = out_ref.shape
        position = place_ref[1] * row_count + lax.broadcasted_iota(jnp.int32, (row_count, 1), 0)
        pair = 2 if prompts % 2 == 0 else 1
        for p in range(0, prompts, pair):
            at = slice(p * row_count, (p + pair) * row_count)
            summed = normed_ref[at, :].astype(jnp.float32) + total[at, :] + down(at)
            finished = normalize(summed, gain_ref[1:2, :], shift_ref[1:2, :])
            for n in range(pair):
                part = finished[n * row_count : (n + 1) * row_count, :]
                inside = position < lengths_ref[p + n]
                out_ref[p + n] = jnp.where(inside, part, 0.0).astype(jnp.bfloat16)


def mlp(lengths, place, normed, whole, order, rows, gain, shift, prompts, chunk):
    count, model_width = normed.shape
    hidden_width = whole.shape[1] // 2
    row_count = count // prompts
    constant = lambda n, *_: (0, 0)
    return pl.pallas_call(
        functools.partial(mlp_kernel, order, rows, chunk),
        out_shape=jax.ShapeDtypeStruct((prompts, row_count, model_width), jnp.bfloat16),
        grid_spec=pltpu.PrefetchScalarGridSpec(
            num_scalar_prefetch=2,
            grid=(hidden_width // chunk + 1,),
            in_specs=[
                pl.BlockSpec((count, model_width), constant),
                pl.BlockSpec(memory_space=pl.ANY),
                pl.BlockSpec(gain.shape, constant),
                pl.BlockSpec(gain.shape, constant),
            ],
            out_specs=pl.BlockSpec((prompts, row_count, model_width), lambda n, *_: (0, 0, 0)),
            scratch_shapes=[
                pltpu.VMEM((2, model_width, chunk), jnp.bfloat16),
                pltpu.VMEM((2, model_width, chunk), jnp.bfloat16),
                pltpu.VMEM((2, count, chunk), jnp.float32),
                pltpu.VMEM((count, model_width), jnp.float32),
                pltpu.SemaphoreType.DMA((2, 2, len(order))),
            ],
        ),
        compiler_params=pltpu.CompilerParams(vmem_limit_bytes=60 * MIB),
        cost_estimate=pl.CostEstimate(
            flops=4 * count * model_width * hidden_width,
            bytes_accessed=4 * model_width * hidden_width + 6 * count * model_width,
            transcendentals=count * hidden_width,
        ),
        name="mlp",
    )(lengths, place, normed, whole, gain, shift)


def shards(tokens, lengths, attn_in, attn_out, mlp_in, mlp_out, norm_gain, norm_shift):
    heads_axis = lax.axis_size("head")
    prompts, seq_len, model_width = tokens.shape
    hidden_width = mlp_in.shape[1]
    width = model_width // heads_axis
    row_count = seq_len // heads_axis
    rows = mlp_in.shape[0]
    place = jnp.stack([lax.axis_index("seq"), lax.axis_index("head")]).astype(jnp.int32)

    def both(start, stop):
        return [mlp_in[:, start:stop], mlp_out.T[:, start:stop]]

    def packed(pieces):
        return jnp.concatenate(pieces, axis=1).astype(jnp.bfloat16)

    in_cast = attn_in.astype(jnp.bfloat16).reshape(rows, 3, heads_axis, width)
    in_cast = in_cast.transpose(2, 0, 1, 3).reshape(heads_axis, rows, 3 * width)
    in_rows = lax.all_to_all(in_cast, "head", 0, 0).reshape(heads_axis * rows, 3 * width)

    whole = gather_cycle(packed(both(0, hidden_width)))
    out_parts = by_depth(attn_out.T.astype(jnp.bfloat16))
    in_parts = by_depth(after(in_rows, out_parts))
    out_blocks = across_second(across_first(out_parts))
    in_parts, arrived = lax.optimization_barrier((in_parts, [block for block, _ in out_blocks]))
    out_blocks = [(block, at) for block, (_, at) in zip(arrived, out_blocks)]
    in_depth = jnp.concatenate(in_parts, axis=0)
    in_blocks = [(in_depth, 0), (swap_seq(in_depth, 1), 1)]

    contexts, caches, count = [], [], prompts // ATTENTION_CALLS
    for start in range(0, prompts, count):
        *caches, own, one, two, three = attention(
            lengths, place, tokens, in_blocks, heads_axis, start, count, caches
        )
        contexts.append([own, swap_head(one, 1), swap_head(two, 2), swap_head(three, 3)])
    out_blocks = other_core(out_blocks)
    normed = project(place, tokens, contexts, out_blocks, norm_gain, norm_shift, rows, 0)
    normed = normed.reshape(prompts * row_count, model_width)
    whole = after(whole, normed)
    order = [s * heads_axis + h for s, h in cycle()]
    encoded = mlp(lengths, place, normed, whole, order, rows, norm_gain, norm_shift, prompts, hidden_width // 4)
    return (encoded, caches[0], caches[1])


def solution(mesh):
    in_specs = (
        P("seq", None, None),
        P("seq"),
        P(("seq", "head"), None, None),
        P(None, ("seq", "head")),
        P(("seq", "head"), None),
        P(None, ("seq", "head")),
        P(),
        P(),
    )
    out_specs = (P("seq", "head", None), P("seq", None, "head"), P("seq", None, "head"))
    return jax.shard_map(shards, mesh=mesh, in_specs=in_specs, out_specs=out_specs, check_vma=False)
```
